128 devices in a mesh: loop: 64 (over z_hi, x, y, core), group: 2 (over z_lo).
Axes of the slice: x: 4, y: 4, z: 4 (z_hi: 2, z_lo: 2; z = z_hi * 2 + z_lo), core: 2. Of those that a mesh axis runs over, the one named last changes fastest.
Arguments:
- references: bfloat16 [262144, 512], P(('loop', 'group')), may hold values from -40 to 40
- bank: bfloat16 [6144, 512], P('loop'), may hold values from -64 to 64
- queries: bfloat16 [1536, 512], P('loop'), may hold values from -64 to 64
Outputs:
- expanded: float32 [1536, 512], P(('loop', 'group'))
The draws below stay inside these ranges and needn't reach their ends.
All inputs are finite; a program needn't handle non-finite values.
Results may differ from the reference program's by a relative error of at most 0.0019.
Values may be sent and summed in bfloat16 or wider, within the bound.
A program may use at most 64 MiB of HBM per device.

```python
import math
import jax
import jax.numpy as jnp
from jax import lax

D = 512
REF_DEV = 2048
REFS = 262144
BANK = 6144
QUERIES = 1536
DEVICES = 128


def column_scale(key, spread):
    raw = jax.random.uniform(jax.random.fold_in(key, 11), (D,), jnp.float32, -spread, spread)
    return jnp.exp(raw) / math.sqrt(math.sinh(2.0 * spread) / (2.0 * spread))


def pairing(key):
    clusters = REFS // 4
    query_target = jax.random.randint(jax.random.fold_in(key, 21), (QUERIES,), 0, REFS)
    source = jax.random.randint(jax.random.fold_in(key, 22), (BANK,), 0, QUERIES)
    member = jax.random.randint(jax.random.fold_in(key, 23), (BANK,), 0, 4)
    anywhere = jax.random.randint(jax.random.fold_in(key, 24), (BANK,), 0, REFS)
    coin = jax.random.randint(jax.random.fold_in(key, 25), (BANK,), 0, 2)
    sibling = query_target[source] % clusters + clusters * member
    bank_target = jnp.where(coin == 1, sibling, anywhere)
    leading = jnp.repeat(query_target[:3], 2)
    bank_target = jnp.concatenate([leading, bank_target[6:]])
    return (query_target, bank_target)


def base_rows(key, index, spread):
    clusters = REFS // 4
    center_key = jax.random.fold_in(key, 12)
    single_key = jax.random.fold_in(key, 13)

    def one_row(row):
        center = jax.random.truncated_normal(jax.random.fold_in(center_key, row % clusters), -4.0, 4.0, (D,), jnp.float32)
        single = jax.random.truncated_normal(jax.random.fold_in(single_key, row), -4.0, 4.0, (D,), jnp.float32)
        return 0.8 * center + 0.6 * single
    return jax.vmap(one_row)(index) * column_scale(key, spread) / math.sqrt(D)


def log_even(key, count, lower, upper):
    return jnp.exp(jax.random.uniform(key, (count,), jnp.float32, math.log(lower), math.log(upper)))


def draw_references(key, part):
    index = jnp.arange(REFS, dtype=jnp.int32)
    spread = 1.151
    return base_rows(key, index, spread).astype(jnp.bfloat16)


def draw_bank(key, part):
    own_key = jax.random.fold_in(key, 7)
    unused, bank_target = pairing(key)
    spread = 1.151
    strength = log_even(jax.random.fold_in(own_key, 1), BANK, 0.6, 2.0)
    noise = jnp.full((BANK,), 0.5, jnp.float32)
    rows = base_rows(key, bank_target, spread)
    extra = jax.random.truncated_normal(jax.random.fold_in(own_key, 2), -4.0, 4.0, (BANK, D), jnp.float32) * column_scale(key, spread) / math.sqrt(D)
    return (math.sqrt(D) * strength[:, None] * (rows + noise[:, None] * extra)).astype(jnp.bfloat16)


def draw_queries(key, part):
    own_key = jax.random.fold_in(key, 5)
    query_target, unused = pairing(key)
    spread = 1.151
    strength = log_even(jax.random.fold_in(own_key, 1), QUERIES, 0.6, 2.0)
    noise = jnp.full((QUERIES,), 0.5, jnp.float32)
    rows = base_rows(key, query_target, spread)
    extra = jax.random.truncated_normal(jax.random.fold_in(own_key, 2), -4.0, 4.0, (QUERIES, D), jnp.float32) * column_scale(key, spread) / math.sqrt(D)
    return (math.sqrt(D) * strength[:, None] * (rows + noise[:, None] * extra)).astype(jnp.bfloat16)


def setup_inputs(seed: int = 0) -> dict:
    splits = jax.random.split(jax.random.key(seed), 4)
    references = draw_references(jax.random.fold_in(splits[3], 71), 0)
    bank = draw_bank(jax.random.fold_in(splits[3], 71), 0)
    queries = draw_queries(jax.random.fold_in(splits[3], 71), 0)
    return dict(references=references, bank=bank, queries=queries)


def similar(rows, columns):
    return lax.dot_general(rows, columns, (((1,), (1,)), ((), ())), preferred_element_type=jnp.float32)

def reference(references, bank, queries):
    blocks = references.reshape(DEVICES, REF_DEV, D)

    def one_block(pooled, block):
        bank_scores = similar(bank, block)
        peak = lax.optimization_barrier(jnp.max(bank_scores, axis=0))
        total = lax.optimization_barrier(jnp.sum(jnp.exp(bank_scores - peak), axis=0))
        offset = peak + jnp.log(total)
        weights = jax.nn.sigmoid(similar(queries, block) - offset).astype(jnp.bfloat16)
        return (pooled + jnp.dot(weights, block, preferred_element_type=jnp.float32), None)
    pooled, unused = lax.scan(one_block, jnp.zeros((QUERIES, D), jnp.float32), blocks)
    scale = lax.rsqrt(lax.optimization_barrier(jnp.mean(pooled * pooled, axis=1, keepdims=True)) + 1e-06)
    return queries.astype(jnp.float32) + pooled * scale
```

```python
import jax
import jax.numpy as jnp
from jax import lax
from jax.experimental import pallas as pl
from jax.experimental.pallas import tpu as pltpu
from jax.sharding import PartitionSpec as P

MESH = pl.DeviceIdType.MESH
SIDE = 4
STEPS = (1, 3, 2)
SLICE = 256
LOW = -1e30
CHUNK_A = {0: 0, 1: 2, 3: 3, 2: 6}
CHUNK_B = {0: 1, 1: 4, 3: 5, 2: 7}
BLOCKS = (2, 1, 3, 0)


def similar(rows, columns):
    return lax.dot_general(
        rows, columns, (((1,), (1,)), ((), ())), preferred_element_type=jnp.float32
    )


def back(distance):
    return (SIDE - distance) % SIDE


def split_rows(rows):
    half = rows.shape[2] // 2
    return jnp.concatenate([rows[:, :, :half], rows[:, :, half:]], axis=1)


def join_rows(rows):
    half = rows.shape[1] // 2
    return jnp.concatenate([rows[:, :half], rows[:, half:]], axis=2)


def kernel(
    refs, bank, queries, out,
    bank_all, own_q, gather_a, gather_b, q_all,
    peak, total, offset, scores, weights,
    pooled, from_sib, send_a, send_b, recv_a, recv_b, sum_a, sum_b, final_a, final_b,
    send_sem, recv_sem,
):
    shard, width = bank.shape
    q_rows = queries.shape[0]
    ref_count = refs.shape[0]
    chunk = 2 * SIDE * shard
    slices = ref_count // SLICE

    index, z_lo = lax.axis_index("loop"), lax.axis_index("group")
    core, y = lax.rem(index, 2), lax.rem(index // 2, SIDE)
    x, z_hi = lax.rem(index // (2 * SIDE), SIDE), index // (2 * SIDE * SIDE)

    def device(dx=0, dy=0, flip_hi=0, flip_lo=0, flip_core=0):
        to_x, to_y = lax.rem(x + dx, SIDE), lax.rem(y + dy, SIDE)
        to_hi = 1 - z_hi if flip_hi else z_hi
        to_lo = 1 - z_lo if flip_lo else z_lo
        to_core = 1 - core if flip_core else core
        return (((to_hi * SIDE + to_x) * SIDE + to_y) * 2 + to_core, to_lo)

    sibling = device(flip_core=1)
    facing = device(flip_hi=1, flip_lo=1)
    along_x = {d: device(dx=d) for d in STEPS}
    along_y = {d: device(dy=d) for d in STEPS}

    moves = {}

    def move(name, src, dst, target):
        k = len(moves)
        moves[name] = pltpu.make_async_remote_copy(
            src_ref=src, dst_ref=dst, send_sem=send_sem.at[k], recv_sem=recv_sem.at[k],
            device_id=target, device_id_type=MESH,
        )

    def bank_at(kind, line, place, count=1, side=0):
        first = (CHUNK_A if kind == "a" else CHUNK_B)[line] * chunk
        first += (side * SIDE + place) * shard
        return bank_all.at[pl.ds(first, count * shard)]

    move("bz", bank, bank_at("b", 0, 0), facing)
    first_ring = {"a": along_x, "b": along_y}
    second_ring = {"a": along_y, "b": along_x}
    gathers = {"a": gather_a, "b": gather_b}
    for kind in "ab":
        own = bank if kind == "a" else bank_at("b", 0, 0)
        for d in STEPS:
            move(f"{kind}1{d}", own, bank_at(kind, 0, back(d)), first_ring[kind][d])
        for place in range(SIDE):
            src = own if place == 0 else bank_at(kind, 0, place)
            for d in (1, 3):
                move(f"{kind}2{place}{d}", src, bank_at(kind, back(d), place), second_ring[kind][d])
        move(f"{kind}r1", bank_at(kind, 1, 0, 2), bank_at(kind, 2, 0, 2), second_ring[kind][3])
        move(f"{kind}r3", bank_at(kind, 3, 2, 2), bank_at(kind, 2, 2, 2), second_ring[kind][1])
        for line in range(SIDE):
            move(f"{kind}s{line}", bank_at(kind, line, 0, SIDE), bank_at(kind, line, 0, SIDE, 1), sibling)
    move("qz", own_q, gather_b.at[0, 0, 0], facing)
    for kind in "ab":
        gather = gathers[kind]
        own = own_q if kind == "a" else gather_b.at[0, 0, 0]
        for d in STEPS:
            move(f"q{kind}1{d}", own, gather.at[0, 0, back(d)], first_ring[kind][d])
            move(f"q{kind}2{d}", gather.at[0, 0], gather.at[back(d), 0], second_ring[kind][d])
        for line in range(SIDE):
            move(f"q{kind}s{line}", gather.at[line, 0], gather.at[line, 1], sibling)
    half = 2 * SIDE * q_rows
    for k in range(SIDE):
        move(f"ps{k}", pooled.at[k, pl.ds(half, half)], from_sib.at[k], sibling)
    for d in STEPS:
        move(f"pa{d}", send_a.at[d - 1], recv_a.at[back(d) - 1], along_y[d])
        move(f"pb{d}", send_b.at[d - 1], recv_b.at[back(d) - 1], along_x[d])
    window = 16
    same_lo = pl.ds(pl.multiple_of(8 * z_lo, 8), window)
    other_lo = pl.ds(pl.multiple_of(8 * (1 - z_lo), 8), window)
    final_devices = []
    for d in range(SIDE):
        for flip in (0, 1):
            rows = other_lo if flip else same_lo
            to_a, to_b = device(dx=d, flip_lo=flip), device(dy=d, flip_hi=1, flip_lo=flip)
            final_devices.append(to_b)
            move(f"fb{d}{flip}", sum_b.at[d, rows], final_b.at[back(d), flip], to_b)
            if d or flip:
                final_devices.append(to_a)
                move(f"fa{d}{flip}", sum_a.at[d, rows], final_a.at[back(d), flip], to_a)

    bank_all[pl.ds(CHUNK_A[0] * chunk, shard), :] = bank[...]
    peak[...] = jnp.full_like(peak, -jnp.inf)
    total[...] = jnp.zeros_like(total)
    scores[1] = jnp.full(scores.shape[1:], LOW, jnp.float32)
    own_q[...] = split_rows(queries[...].astype(jnp.float32)[None])[0].astype(jnp.bfloat16)
    gather_a[0, 0, 0] = own_q[...]

    partners = [sibling, *along_y.values(), *final_devices]
    barrier = pltpu.get_barrier_semaphore()
    for partner in partners:
        pl.semaphore_signal(barrier, inc=1, device_id=partner, device_id_type=MESH)
    pl.semaphore_wait(barrier, len(partners))

    def start(*names):
        for name in names:
            moves[name].start()

    def arrived(*names):
        for name in names:
            moves[name].wait_recv()

    def at_start():
        start("bz", "a11", "a13", "a12", "a201", "a203")
        arrived("bz")
        start("b11", "b13", "b12", "b201", "b203")
        for d in STEPS:
            arrived(f"a1{d}")
            start(f"a2{back(d)}1", f"a2{back(d)}3")
        start("as0")
        for d in STEPS:
            arrived(f"b1{d}")
            start(f"b2{back(d)}1", f"b2{back(d)}3")
        start("bs0")
        start("qz", "qa11", "qa13", "qa12")
        arrived("as0")

    def pass_on(kind, line):
        arrived(*[f"{kind}2{place}{back(line)}" for place in range(SIDE)])
        start(f"{kind}r{line}", f"{kind}s{line}")

    def before_b0():
        arrived("bs0")
        arrived("qz")
        start("qb11", "qb13", "qb12")

    def before_a1():
        pass_on("a", 1)
        pass_on("a", 3)
        pass_on("b", 1)
        pass_on("b", 3)
        arrived("qa11", "qa13", "qa12")
        start("qa21", "qa23", "qa22", "qas0")
        arrived("qb11", "qb13", "qb12")
        start("qb21", "qb23", "qb22", "qbs0")
        arrived("as1")

    def before_b3():
        arrived("bs3")
        arrived("ar1", "ar3")
        start("as2")
        arrived("br1", "br3")
        start("bs2")

    def before_a2():
        arrived("as2")
        for d in STEPS:
            arrived(f"qa2{d}", f"qb2{d}")
            start(f"qas{back(d)}", f"qbs{back(d)}")

    events = (
        at_start, before_b0, before_a1, lambda: arrived("as3"), lambda: arrived("bs1"),
        before_b3, before_a2, lambda: arrived("bs2"),
    )

    def absorb(slot, piece):
        tile = scores[slot].reshape(chunk // 8, 8, SLICE)
        columns = slice(piece * SLICE, (piece + 1) * SLICE)
        old = peak[:, columns]
        new = jnp.maximum(old, jnp.max(tile, axis=0))
        added = jnp.sum(jnp.exp(tile - new[None]), axis=0)
        total[:, columns] = total[:, columns] * jnp.exp(old - new) + added
        peak[:, columns] = new

    def one_chunk(i, carry):
        for k, event in enumerate(events):
            pl.when(i == k)(event)
        rows = pl.ds(pl.multiple_of(i * chunk, chunk), chunk)
        for piece in range(slices):
            scores[piece % 2] = similar(bank_all[rows, :], refs[piece * SLICE:(piece + 1) * SLICE, :])
            absorb((piece + 1) % 2, (piece - 1) % slices)
        return carry

    lax.fori_loop(0, len(events), one_chunk, 0)
    absorb((slices - 1) % 2, slices - 1)
    highest = jnp.max(peak[...], axis=0, keepdims=True)
    summed = jnp.sum(total[...] * jnp.exp(peak[...] - highest), axis=0, keepdims=True)
    offset[...] = jnp.broadcast_to(highest + jnp.log(summed), offset.shape)

    for d in range(SIDE):
        arrived(f"qas{d}", f"qbs{d}")
    quarter = SIDE * q_rows
    for k, line in enumerate(BLOCKS):
        for j, gather in enumerate((gather_a, gather_b)):
            for side in range(2):
                rows = join_rows(gather[line, side].astype(jnp.float32))
                first = (2 * side + j) * quarter
                q_all[k, first:first + quarter, :] = rows.reshape(quarter, width).astype(jnp.bfloat16)

    def pool(k, carry):
        block = q_all[k]
        for piece in range(slices):
            columns = slice(piece * SLICE, (piece + 1) * SLICE)
            tile = similar(block, refs[columns, :]).reshape(2 * half // 8, 8, SLICE)
            tile = 1.0 / (1.0 + jnp.exp(offset[:, columns][None] - tile))
            weights[:, columns] = tile.reshape(2 * half, SLICE).astype(jnp.bfloat16)
        pooled[k] = jnp.dot(weights[...], refs[...], preferred_element_type=jnp.float32)
        for j in range(SIDE):
            pl.when(k == j)(lambda j=j: after_pool(j))
        return carry

    def after_pool(k):
        start(f"ps{k}")
        if k >= 1:
            reduce_block(k - 1)

    def reduce_block(k):
        arrived(f"ps{k}")
        sums = pooled[k, :half, :] + from_sib[k]
        line = BLOCKS[k]
        for j, send in enumerate((send_a, send_b)):
            rows = sums[j * quarter:(j + 1) * quarter].reshape(SIDE, q_rows, width)
            send[line - 1] = split_rows(rows).astype(jnp.bfloat16)
        start(f"pa{line}", f"pb{line}")

    lax.fori_loop(0, SIDE, pool, 0)
    last = SIDE - 1
    arrived(f"ps{last}")
    sums = pooled[last, :half, :] + from_sib[last]
    for j, (name, recv, result) in enumerate((("pa", recv_a, sum_a), ("pb", recv_b, sum_b))):
        rows = sums[j * quarter:(j + 1) * quarter].reshape(SIDE, q_rows, width)
        for d in STEPS:
            arrived(f"{name}{d}")
            rows = rows + join_rows(recv[back(d) - 1].astype(jnp.float32))
        result[...] = rows
    sends = [name for name in moves if name.startswith("f")]
    start(*sends)
    rows = sum_a[0, same_lo, :]
    own = jnp.where(z_lo == 0, queries[...].astype(jnp.float32)[:window], queries[...].astype(jnp.float32)[8:])
    for name in sends:
        arrived(name)
        kind, d, flip = name[1], int(name[2]), int(name[3])
        rows = rows + (final_a if kind == "a" else final_b)[back(d), flip]
    scale = lax.rsqrt(jnp.mean(rows * rows, axis=1, keepdims=True) + 1e-06)
    result = own + rows * scale
    count = out.shape[0]
    out[...] = jnp.where(z_lo == 0, result[:count], result[window - count:])
    for copy in moves.values():
        copy.wait_send()


MOVES = 180


def per_device(references, bank, queries):
    ref_count, width = references.shape
    shard, q_rows = bank.shape[0], queries.shape[0]
    chunk = 2 * SIDE * shard
    block = 4 * SIDE * q_rows
    unit = (2 * q_rows, width // 2)
    f32, bf16 = jnp.float32, jnp.bfloat16
    return pl.pallas_call(
        kernel,
        out_shape=jax.ShapeDtypeStruct((q_rows // 2, width), f32),
        in_specs=[pl.BlockSpec(memory_space=pltpu.VMEM)] * 3,
        out_specs=pl.BlockSpec(memory_space=pltpu.VMEM),
        scratch_shapes=[
            pltpu.VMEM((2 * SIDE * chunk, width), bf16),
            pltpu.VMEM(unit, bf16),
            pltpu.VMEM((SIDE, 2, SIDE, *unit), bf16),
            pltpu.VMEM((SIDE, 2, SIDE, *unit), bf16),
            pltpu.VMEM((SIDE, block, width), bf16),
            pltpu.VMEM((8, ref_count), f32),
            pltpu.VMEM((8, ref_count), f32),
            pltpu.VMEM((8, ref_count), f32),
            pltpu.VMEM((2, chunk, SLICE), f32),
            pltpu.VMEM((block, ref_count), bf16),
            pltpu.VMEM((SIDE, block, width), f32),
            pltpu.VMEM((SIDE, block // 2, width), f32),
            pltpu.VMEM((SIDE - 1, SIDE, *unit), bf16),
            pltpu.VMEM((SIDE - 1, SIDE, *unit), bf16),
            pltpu.VMEM((SIDE - 1, SIDE, *unit), bf16),
            pltpu.VMEM((SIDE - 1, SIDE, *unit), bf16),
            pltpu.VMEM((SIDE, q_rows, width), f32),
            pltpu.VMEM((SIDE, q_rows, width), f32),
            pltpu.VMEM((SIDE, 2, 16, width), f32),
            pltpu.VMEM((SIDE, 2, 16, width), f32),
            pltpu.SemaphoreType.DMA((MOVES,)),
            pltpu.SemaphoreType.DMA((MOVES,)),
        ],
        compiler_params=pltpu.CompilerParams(
            collective_id=0, has_side_effects=True, vmem_limit_bytes=56 * 2**20
        ),
    )(references, bank, queries)


def solution(mesh):
    return jax.shard_map(
        per_device,
        mesh=mesh,
        in_specs=(P(("loop", "group"), None), P("loop", None), P("loop", None)),
        out_specs=P(("loop", "group"), None),
        check_vma=False,
    )
```

```python
import jax
import jax.numpy as jnp
from jax import lax
from jax.experimental import pallas as pl
from jax.experimental.pallas import tpu as pltpu
from jax.sharding import PartitionSpec as P

MESH = pl.DeviceIdType.MESH
SIDE = 4
STEPS = (1, 3, 2)
SLICE = 256
LOW = -1e30
BLOCKS = (2, 1, 3, 0)


def similar(rows, columns):
    return lax.dot_general(
        rows, columns, (((1,), (1,)), ((), ())), preferred_element_type=jnp.float32
    )


def back(distance):
    return (SIDE - distance) % SIDE


def split_rows(rows):
    half = rows.shape[2] // 2
    return jnp.concatenate([rows[:, :, :half], rows[:, :, half:]], axis=1)


def join_rows(rows):
    half = rows.shape[1] // 2
    return jnp.concatenate([rows[:, :half], rows[:, half:]], axis=2)


PARTS = (
    ("a00", "b00", "a10", "a30"),
    ("a01", "a03", "b01", "b03"),
    ("a20", "b02", "b10", "b30"),
    ("a11", "a13", "b11", "b31"),
    ("a02", "b20", "near a2", "near b2"),
    ("a31", "a33", "b13", "b33"),
    ("a21", "a23", "b12", "b32"),
    ("a22", "b22", "far a2", "far b2"),
)
SLOTS = {name: (k, j) for k, names in enumerate(PARTS) for j, name in enumerate(names)}
UNITS = 4
WINDOW = 16
SEND_SEMS, RECV_SEMS = 12, 40


def kernel(
    refs_hbm, bank, queries, out,
    refs, bank_all, own_q, gather_a, gather_b, q_all,
    peak, total, offset, scores, weights,
    pooled, from_sib, send_a, send_b, recv_a, recv_b, sums, windows, final,
    load_sem, send_sem, recv_sem,
):
    shard, width = bank.shape
    q_rows = queries.shape[0]
    ref_count = refs.shape[0]
    part = UNITS * shard
    chunk = 2 * part
    slices = ref_count // SLICE

    load = pltpu.make_async_copy(refs_hbm, refs, load_sem)
    load.start()

    index, z_lo = lax.axis_index("loop"), lax.axis_index("group")
    core, y = lax.rem(index, 2), lax.rem(index // 2, SIDE)
    x, z_hi = lax.rem(index // (2 * SIDE), SIDE), index // (2 * SIDE * SIDE)

    def device(dx=0, dy=0, flip_hi=0, flip_lo=0, flip_core=0):
        to_x, to_y = lax.rem(x + dx, SIDE), lax.rem(y + dy, SIDE)
        to_hi = 1 - z_hi if flip_hi else z_hi
        to_lo = 1 - z_lo if flip_lo else z_lo
        to_core = 1 - core if flip_core else core
        return (((to_hi * SIDE + to_x) * SIDE + to_y) * 2 + to_core, to_lo)

    sibling = device(flip_core=1)
    twin = device(flip_lo=1)
    facing = device(flip_hi=1, flip_lo=1)
    along_x = {d: device(dx=d) for d in STEPS}
    along_y = {d: device(dy=d) for d in STEPS}

    moves, send_groups, recv_groups = {}, {}, {}

    def group_sem(sems, groups, name):
        return sems.at[groups.setdefault(name, len(groups))]

    def copy(src, dst, sent, landed, target):
        return pltpu.make_async_remote_copy(
            src_ref=src, dst_ref=dst,
            send_sem=group_sem(send_sem, send_groups, sent), recv_sem=group_sem(recv_sem, recv_groups, landed),
            device_id=target, device_id_type=MESH,
        )

    def move(name, src, dst, sent, landed, target):
        moves[name] = lambda: copy(src, dst, sent, landed, target)

    def start(*names):
        for name in names:
            moves[name]().start()

    def arrived(landed, what):
        copy(what, what, next(iter(send_groups)), landed, sibling).wait_recv()

    def all_sent(sent, what):
        copy(what, what, sent, next(iter(recv_groups)), sibling).wait_send()

    def first_row(k, side=0):
        return min((k + 1) * chunk, len(PARTS) * chunk - part) if side else max(k * chunk - part, 0)

    def unit(name):
        k, j = SLOTS[name]
        return bank_all.at[pl.ds(first_row(k) + j * shard, shard)]

    def whole_part(k, side=0):
        return bank_all.at[pl.ds(first_row(k, side), part)]

    def pair(name):
        k, j = SLOTS[name]
        return bank_all.at[pl.ds(first_row(k) + j * shard, 2 * shard)]

    unit_sends = []

    def send_unit(name, src, dst, landed, target):
        move(name, src, unit(dst), f"u{len(unit_sends) // 16}", landed, target)
        unit_sends.append(name)

    send_unit("z", bank, "b00", "z", facing)
    for d in STEPS:
        send_unit(f"a1{d}", bank, f"a{back(d)}0", f"a1{d}", along_x[d])
        send_unit(f"b1{d}", unit("b00"), f"b0{back(d)}", f"b1{d}", along_y[d])
    for place, k_a, k_b in ((0, 1, 2), (1, 3, 3), (3, 5, 5), (2, 6, 6)):
        for d in (1, 3):
            send_unit(f"a2{place}{d}", unit(f"a{place}0") if place else bank, f"a{place}{back(d)}", f"c{k_a}", along_y[d])
            send_unit(f"b2{place}{d}", unit(f"b0{place}"), f"b{back(d)}{place}", f"c{k_b}", along_x[d])

    def near(names):
        k, j = SLOTS[names[0]]
        return bank_all.at[pl.ds(pl.multiple_of(first_row(k) + (j + z_lo) * shard, shard), shard)]

    send_unit("a2n", near(("a10", "a30")), "near a2", "c4", along_y[2])
    send_unit("b2n", near(("b01", "b03")), "near b2", "c4", along_x[2])
    send_unit("za", unit("b02"), "a02", "c4", facing)
    send_unit("zb", unit("a20"), "b20", "c4", facing)
    send_unit("a222", unit("a20"), "a22", "c7", along_y[2])
    send_unit("b222", unit("b02"), "b22", "c7", along_x[2])
    send_unit("ta", unit("near a2"), "far a2", "c7", twin)
    send_unit("tb", unit("near b2"), "far b2", "c7", twin)
    for k in range(len(PARTS)):
        move(f"s{k}", whole_part(k), whole_part(k, 1), f"s{k // 4}", f"s{k}", sibling)

    first_ring = {"a": along_x, "b": along_y}
    second_ring = {"a": along_y, "b": along_x}
    gathers = {"a": gather_a, "b": gather_b}
    plane = SIDE * SIDE
    move("qz", own_q, gather_b.at[0], "q", "qz", facing)
    for kind, gather in gathers.items():
        own = own_q if kind == "a" else gather_b.at[0]
        for d in STEPS:
            move(f"q{kind}1{d}", own, gather.at[back(d)], "q", f"q{kind}1", first_ring[kind][d])
            move(f"q{kind}2{d}", gather.at[pl.ds(0, SIDE)], gather.at[pl.ds(back(d) * SIDE, SIDE)], "q", f"q{kind}2",
                 second_ring[kind][d])
        for name, first, count in (("0", 0, SIDE), ("3", SIDE, plane - SIDE)):
            move(f"q{kind}s{name}", gather.at[pl.ds(first, count)], gather.at[pl.ds(plane + first, count)], "qs",
                 f"q{kind}s{name}", sibling)

    half = 2 * SIDE * q_rows
    for k in range(SIDE):
        move(f"p{k}", pooled.at[k, pl.ds(half, half)], from_sib.at[k], "p", f"p{k}", sibling)
    for d in STEPS:
        move(f"pa{d}", send_a.at[d - 1], recv_a.at[back(d) - 1], "pa", "pa", along_y[d])
        move(f"pb{d}", send_b.at[d - 1], recv_b.at[back(d) - 1], "pb", "pb", along_x[d])
    ends = []
    for d in range(SIDE):
        for flip in (0, 1):
            for j, target in enumerate((device(dx=d, flip_lo=flip), device(dy=d, flip_hi=1, flip_lo=flip))):
                if d or flip or j:
                    place = (flip * 2 + j) * SIDE
                    move(f"f{place + d}", windows.at[place + d], final.at[place + back(d)], "f", "f", target)
                    ends.append(f"f{place + d}")

    bank_all[pl.ds(0, shard), :] = bank[...]
    peak[...] = jnp.full_like(peak, -jnp.inf)
    total[...] = jnp.zeros_like(total)
    scores[1] = jnp.full(scores.shape[1:], LOW, jnp.float32)
    own_q[...] = split_rows(queries[...].astype(jnp.float32)[None])[0].astype(jnp.bfloat16)
    gather_a[0] = own_q[...]

    partners = [sibling, twin, facing, device(flip_hi=1), *along_x.values(), *along_y.values()]
    barrier = pltpu.get_barrier_semaphore()
    for partner in partners:
        pl.semaphore_signal(barrier, inc=1, device_id=partner, device_id_type=MESH)
    pl.semaphore_wait(barrier, len(partners))

    def from_own(k):
        arrived(f"c{k}", whole_part(k))
        start(f"s{k}")

    def from_other(k):
        arrived(f"s{k}", whole_part(k, 1))

    def before_1():
        for d, place in ((1, 3), (3, 1)):
            arrived(f"b1{d}", unit(f"b0{place}"))
        start("a211", "a213", "b211", "b213")
        arrived("a12", unit("a20"))
        start("zb")
        arrived("c1", pair("a01"))
        start("s1", "qz")
        from_other(0)

    def before_2():
        arrived("b12", unit("b02"))
        start("a2n", "b2n", "za")
        arrived("c2", pair("b10"))
        start("s2", "qa11", "qa13", "qa12")
        from_other(1)

    def before_3():
        start("a231", "a233", "b231", "b233")
        from_own(3)
        arrived("qz", gather_b.at[0])
        start("qb11", "qb13", "qb12")
        from_other(2)

    def before_4():
        from_own(4)
        start("a221", "a223", "b221", "b223", "ta", "tb")
        from_other(3)

    def before_5():
        start("a222", "b222")
        from_own(5)
        arrived("qa1", gather_a.at[pl.ds(1, SIDE - 1)])
        arrived("qb1", gather_b.at[pl.ds(1, SIDE - 1)])
        start("qa22", "qb22", "qas0", "qbs0")
        from_other(4)

    def before_6():
        start("qa21", "qa23", "qb21", "qb23")
        from_own(6)
        from_other(5)

    def before_7():
        from_own(7)
        from_other(6)

    events = (before_1, before_2, before_3, before_4, before_5, before_6, before_7)

    def absorb(slot, piece, count=chunk):
        tile = scores[slot, :count].reshape(count // 8, 8, SLICE)
        columns = slice(piece * SLICE, (piece + 1) * SLICE)
        old = peak[:, columns]
        new = jnp.maximum(old, jnp.max(tile, axis=0))
        added = jnp.sum(jnp.exp(tile - new[None]), axis=0)
        total[:, columns] = total[:, columns] * jnp.exp(old - new) + added
        peak[:, columns] = new

    def score(first, count, before=chunk):
        rows = pl.ds(first, count)
        for piece in range(slices):
            scores[piece % 2, :count] = similar(bank_all[rows, :], refs[piece * SLICE:(piece + 1) * SLICE, :])
            absorb((piece + 1) % 2, (piece - 1) % slices, count if piece else before)

    start("z", "a11", "a13", "a201", "a203", "a12")
    arrived("z", unit("b00"))
    start("b11", "b13")
    for d, place in ((1, 3), (3, 1)):
        arrived(f"a1{d}", unit(f"a{place}0"))
    start("b201", "b203", "b12", "s0")
    load.wait()
    score(0, part)

    def one_chunk(i, carry):
        for k, event in enumerate(events):
            pl.when(i == k)(event)
        score(pl.multiple_of(part + i * chunk, part), chunk)
        return carry

    lax.fori_loop(0, len(events), one_chunk, 0)
    rest = pl.ds(SIDE, plane - SIDE)
    for kind, gather in gathers.items():
        arrived(f"q{kind}2", gather.at[rest])
        start(f"q{kind}s3")
    from_other(len(PARTS) - 1)
    score(first_row(len(PARTS) - 1, 1), part)
    absorb((slices - 1) % 2, slices - 1, part)
    highest = jnp.max(peak[...], axis=0, keepdims=True)
    summed = jnp.sum(total[...] * jnp.exp(peak[...] - highest), axis=0, keepdims=True)
    offset[...] = jnp.broadcast_to(highest + jnp.log(summed), offset.shape)

    quarter = SIDE * q_rows
    for kind, gather in gathers.items():
        arrived(f"q{kind}s0", gather.at[pl.ds(plane, SIDE)])
        arrived(f"q{kind}s3", gather.at[pl.ds(plane + SIDE, plane - SIDE)])
    for k, line in enumerate(BLOCKS):
        for j, gather in enumerate((gather_a, gather_b)):
            for side in range(2):
                first = side * plane + line * SIDE
                rows = join_rows(gather[first:first + SIDE].astype(jnp.float32))
                first = (2 * side + j) * quarter
                q_all[k, first:first + quarter, :] = rows.reshape(quarter, width).astype(jnp.bfloat16)

    def pool(k, carry):
        block = q_all[k]
        for piece in range(slices):
            columns = slice(piece * SLICE, (piece + 1) * SLICE)
            tile = similar(block, refs[columns, :]).reshape(2 * half // 8, 8, SLICE)
            tile = 1.0 / (1.0 + jnp.exp(offset[:, columns][None] - tile))
            weights[:, columns] = tile.reshape(2 * half, SLICE).astype(jnp.bfloat16)
        pooled[k] = jnp.dot(weights[...], refs[...], preferred_element_type=jnp.float32)
        for j in range(SIDE):
            pl.when(k == j)(lambda j=j: after_pool(j))
        return carry

    def after_pool(k):
        start(f"p{k}")
        if k >= 1:
            reduce_block(k - 1)

    def both_cores(k):
        arrived(f"p{k}", from_sib.at[k])
        rows = pooled[k, :half, :] + from_sib[k]
        return [rows[j * quarter:(j + 1) * quarter].reshape(SIDE, q_rows, width) for j in range(2)]

    def reduce_block(k):
        line = BLOCKS[k]
        for rows, send in zip(both_cores(k), (send_a, send_b)):
            send[line - 1] = split_rows(rows).astype(jnp.bfloat16)
        start(f"pa{line}", f"pb{line}")

    lax.fori_loop(0, SIDE, pool, 0)
    same_lo = pl.ds(pl.multiple_of(8 * z_lo, 8), WINDOW)
    other_lo = pl.ds(pl.multiple_of(8 * (1 - z_lo), 8), WINDOW)
    for j, (rows, recv) in enumerate(zip(both_cores(SIDE - 1), (recv_a, recv_b))):
        arrived("pa" if j == 0 else "pb", recv)
        sums[j] = rows + sum(join_rows(recv[d].astype(jnp.float32)) for d in range(SIDE - 1))
        for flip, lo in enumerate((same_lo, other_lo)):
            first = (flip * 2 + j) * SIDE
            windows[first:first + SIDE] = sums[j, :, lo, :].astype(jnp.bfloat16)
    start(*ends)
    rows = sums[0, 0, same_lo, :]
    own = queries[...].astype(jnp.float32)
    own = jnp.where(z_lo == 0, own[:WINDOW], own[q_rows - WINDOW:])
    arrived("f", final.at[pl.ds(1, 4 * SIDE - 1)])
    rows = rows + jnp.sum(final[1:].astype(jnp.float32), axis=0)
    scale = lax.rsqrt(jnp.mean(rows * rows, axis=1, keepdims=True) + 1e-06)
    result = own + rows * scale
    count = out.shape[0]
    out[...] = jnp.where(z_lo == 0, result[:count], result[WINDOW - count:])

    all_sent("u0", bank_all.at[pl.ds(0, 16 * shard)])
    all_sent("u1", bank_all.at[pl.ds(0, (len(unit_sends) - 16) * shard)])
    all_sent("s0", bank_all.at[pl.ds(0, 4 * part)])
    all_sent("s1", bank_all.at[pl.ds(0, 4 * part)])
    all_sent("q", gather_a.at[pl.ds(0, 2 * plane - 1)])
    all_sent("qs", gather_a)
    all_sent("p", from_sib)
    all_sent("pa", send_a)
    all_sent("pb", send_b)
    all_sent("f", final.at[pl.ds(1, 4 * SIDE - 1)])


def per_device(references, bank, queries):
    ref_count, width = references.shape
    shard, q_rows = bank.shape[0], queries.shape[0]
    chunk = 2 * UNITS * shard
    block = 4 * SIDE * q_rows
    unit = (2 * q_rows, width // 2)
    f32, bf16 = jnp.float32, jnp.bfloat16
    return pl.pallas_call(
        kernel,
        out_shape=jax.ShapeDtypeStruct((q_rows // 2, width), f32),
        in_specs=[
            pl.BlockSpec(memory_space=pl.ANY),
            pl.BlockSpec(memory_space=pltpu.VMEM),
            pl.BlockSpec(memory_space=pltpu.VMEM),
        ],
        out_specs=pl.BlockSpec(memory_space=pltpu.VMEM),
        scratch_shapes=[
            pltpu.VMEM((ref_count, width), bf16),
            pltpu.VMEM((len(PARTS) * chunk, width), bf16),
            pltpu.VMEM(unit, bf16),
            pltpu.VMEM((2 * SIDE * SIDE, *unit), bf16),
            pltpu.VMEM((2 * SIDE * SIDE, *unit), bf16),
            pltpu.VMEM((SIDE, block, width), bf16),
            pltpu.VMEM((8, ref_count), f32),
            pltpu.VMEM((8, ref_count), f32),
            pltpu.VMEM((8, ref_count), f32),
            pltpu.VMEM((2, chunk, SLICE), f32),
            pltpu.VMEM((block, ref_count), bf16),
            pltpu.VMEM((SIDE, block, width), f32),
            pltpu.VMEM((SIDE, block // 2, width), f32),
            pltpu.VMEM((SIDE - 1, SIDE, *unit), bf16),
            pltpu.VMEM((SIDE - 1, SIDE, *unit), bf16),
            pltpu.VMEM((SIDE - 1, SIDE, *unit), bf16),
            pltpu.VMEM((SIDE - 1, SIDE, *unit), bf16),
            pltpu.VMEM((2, SIDE, q_rows, width), f32),
            pltpu.VMEM((4 * SIDE, WINDOW, width), bf16),
            pltpu.VMEM((4 * SIDE, WINDOW, width), bf16),
            pltpu.SemaphoreType.DMA,
            pltpu.SemaphoreType.DMA((SEND_SEMS,)),
            pltpu.SemaphoreType.DMA((RECV_SEMS,)),
        ],
        compiler_params=pltpu.CompilerParams(
            collective_id=0, has_side_effects=True, vmem_limit_bytes=56 * 2**20
        ),
    )(references, bank, queries)


def solution(mesh):
    return jax.shard_map(
        per_device,
        mesh=mesh,
        in_specs=(P(("loop", "group"), None), P("loop", None), P("loop", None)),
        out_specs=P(("loop", "group"), None),
        check_vma=False,
    )
```

```python
import jax
import jax.numpy as jnp
from jax import lax
from jax.experimental import pallas as pl
from jax.experimental.pallas import tpu as pltpu
from jax.sharding import PartitionSpec as P

MESH = pl.DeviceIdType.MESH
SIDE = 4
STEPS = (1, 3, 2)
SLICE = 256
LOW = -1e30
BLOCKS = (2, 1, 3, 0)


def similar(rows, columns):
    return lax.dot_general(
        rows, columns, (((1,), (1,)), ((), ())), preferred_element_type=jnp.float32
    )


def back(distance):
    return (SIDE - distance) % SIDE


def split_rows(rows):
    half = rows.shape[2] // 2
    return jnp.concatenate([rows[:, :, :half], rows[:, :, half:]], axis=1)


def join_rows(rows):
    half = rows.shape[1] // 2
    return jnp.concatenate([rows[:, :half], rows[:, half:]], axis=2)


PARTS = (
    ("a00", "b00", "a10", "a30"),
    ("a01", "a03", "b01", "b03"),
    ("a20", "b02", "b10", "b30"),
    ("a11", "a13", "b11", "b31"),
    ("a02", "b20", "near a2", "near b2"),
    ("a31", "a33", "b13", "b33"),
    ("a21", "a23", "b12", "b32"),
    ("a22", "b22", "far a2", "far b2"),
)
SLOTS = {name: (k, j) for k, names in enumerate(PARTS) for j, name in enumerate(names)}
UNITS = 4
WINDOW = 16
SEND_SEMS, RECV_SEMS = 12, 40


def kernel(
    refs_hbm, bank, queries, out,
    refs, bank_all, own_q, gather_a, gather_b, q_all,
    peak, total, offset, scores, weights,
    pooled, from_sib, send_a, send_b, recv_a, recv_b, sums, windows, final,
    load_sem, send_sem, recv_sem,
):
    shard, width = bank.shape
    q_rows = queries.shape[0]
    ref_count = refs.shape[0]
    part = UNITS * shard
    chunk = 2 * part
    slices = ref_count // SLICE

    load = pltpu.make_async_copy(refs_hbm, refs, load_sem)
    load.start()

    index, z_lo = lax.axis_index("loop"), lax.axis_index("group")
    core, y = lax.rem(index, 2), lax.rem(index // 2, SIDE)
    x, z_hi = lax.rem(index // (2 * SIDE), SIDE), index // (2 * SIDE * SIDE)

    def device(dx=0, dy=0, flip_hi=0, flip_lo=0, flip_core=0):
        to_x, to_y = lax.rem(x + dx, SIDE), lax.rem(y + dy, SIDE)
        to_hi = 1 - z_hi if flip_hi else z_hi
        to_lo = 1 - z_lo if flip_lo else z_lo
        to_core = 1 - core if flip_core else core
        return (((to_hi * SIDE + to_x) * SIDE + to_y) * 2 + to_core, to_lo)

    sibling = device(flip_core=1)
    twin = device(flip_lo=1)
    facing = device(flip_hi=1, flip_lo=1)
    along_x = {d: device(dx=d) for d in STEPS}
    along_y = {d: device(dy=d) for d in STEPS}

    moves, send_groups, recv_groups = {}, {}, {}

    def group_sem(sems, groups, name):
        return sems.at[groups.setdefault(name, len(groups))]

    def copy(src, dst, sent, landed, target):
        return pltpu.make_async_remote_copy(
            src_ref=src, dst_ref=dst,
            send_sem=group_sem(send_sem, send_groups, sent), recv_sem=group_sem(recv_sem, recv_groups, landed),
            device_id=target, device_id_type=MESH,
        )

    def move(name, src, dst, sent, landed, target):
        moves[name] = lambda: copy(src, dst, sent, landed, target)

    def start(*names):
        for name in names:
            moves[name]().start()

    def arrived(landed, what):
        copy(what, what, next(iter(send_groups)), landed, sibling).wait_recv()

    def all_sent(sent, what):
        copy(what, what, sent, next(iter(recv_groups)), sibling).wait_send()

    def first_row(k, side=0):
        return min((k + 1) * chunk, len(PARTS) * chunk - part) if side else max(k * chunk - part, 0)

    def unit(name):
        k, j = SLOTS[name]
        return bank_all.at[pl.ds(first_row(k) + j * shard, shard)]

    def whole_part(k, side=0):
        return bank_all.at[pl.ds(first_row(k, side), part)]

    def pair(name):
        k, j = SLOTS[name]
        return bank_all.at[pl.ds(first_row(k) + j * shard, 2 * shard)]

    unit_sends = []

    def send_unit(name, src, dst, landed, target):
        move(name, src, unit(dst), f"u{len(unit_sends) // 16}", landed, target)
        unit_sends.append(name)

    send_unit("z", bank, "b00", "z", facing)
    for d in STEPS:
        send_unit(f"a1{d}", bank, f"a{back(d)}0", f"a1{d}", along_x[d])
        send_unit(f"b1{d}", unit("b00"), f"b0{back(d)}", f"b1{d}", along_y[d])
    for place, k_a, k_b in ((0, 1, 2), (1, 3, 3), (3, 5, 5), (2, 6, 6)):
        for d in (1, 3):
            send_unit(f"a2{place}{d}", unit(f"a{place}0") if place else bank, f"a{place}{back(d)}", f"c{k_a}", along_y[d])
            send_unit(f"b2{place}{d}", unit(f"b0{place}"), f"b{back(d)}{place}", f"c{k_b}", along_x[d])

    def near(names):
        k, j = SLOTS[names[0]]
        return bank_all.at[pl.ds(pl.multiple_of(first_row(k) + (j + z_lo) * shard, shard), shard)]

    send_unit("a2n", near(("a10", "a30")), "near a2", "c4", along_y[2])
    send_unit("b2n", near(("b01", "b03")), "near b2", "c4", along_x[2])
    send_unit("za", unit("b02"), "a02", "c4", facing)
    send_unit("zb", unit("a20"), "b20", "c4", facing)
    send_unit("a222", unit("a20"), "a22", "c7", along_y[2])
    send_unit("b222", unit("b02"), "b22", "c7", along_x[2])
    send_unit("ta", unit("near a2"), "far a2", "c7", twin)
    send_unit("tb", unit("near b2"), "far b2", "c7", twin)
    for k in range(len(PARTS)):
        move(f"s{k}", whole_part(k), whole_part(k, 1), f"s{k // 4}", f"s{k}", sibling)

    first_ring = {"a": along_x, "b": along_y}
    second_ring = {"a": along_y, "b": along_x}
    gathers = {"a": gather_a, "b": gather_b}
    plane = SIDE * SIDE
    move("qz", own_q, gather_b.at[0], "q", "qz", facing)
    for kind, gather in gathers.items():
        own = own_q if kind == "a" else gather_b.at[0]
        for d in STEPS:
            move(f"q{kind}1{d}", own, gather.at[back(d)], "q", f"q{kind}1", first_ring[kind][d])
            move(f"q{kind}2{d}", gather.at[pl.ds(0, SIDE)], gather.at[pl.ds(back(d) * SIDE, SIDE)], "q", f"q{kind}2",
                 second_ring[kind][d])
        for name, first, count in (("0", 0, SIDE), ("3", SIDE, plane - SIDE)):
            move(f"q{kind}s{name}", gather.at[pl.ds(first, count)], gather.at[pl.ds(plane + first, count)], "qs",
                 f"q{kind}s{name}", sibling)

    half = 2 * SIDE * q_rows
    for k in range(SIDE):
        move(f"p{k}", pooled.at[k, pl.ds(half, half)], from_sib.at[k], "p", f"p{k}", sibling)
    for d in STEPS:
        move(f"pa{d}", send_a.at[d - 1], recv_a.at[back(d) - 1], "pa", "pa", along_y[d])
        move(f"pb{d}", send_b.at[d - 1], recv_b.at[back(d) - 1], "pb", "pb", along_x[d])
    ends = []
    for d in range(SIDE):
        for flip in (0, 1):
            for j, target in enumerate((device(dx=d, flip_lo=flip), device(dy=d, flip_hi=1, flip_lo=flip))):
                if d or flip or j:
                    place = (flip * 2 + j) * SIDE
                    move(f"f{place + d}", windows.at[place + d], final.at[place + back(d)], "f", "f", target)
                    ends.append(f"f{place + d}")

    bank_all[pl.ds(0, shard), :] = bank[...]
    peak[...] = jnp.full_like(peak, -jnp.inf)
    total[...] = jnp.zeros_like(total)
    scores[1] = jnp.full(scores.shape[1:], LOW, jnp.float32)
    own_q[...] = split_rows(queries[...].astype(jnp.float32)[None])[0].astype(jnp.bfloat16)
    gather_a[0] = own_q[...]

    partners = [sibling, twin, facing, device(flip_hi=1), *along_x.values(), *along_y.values()]
    barrier = pltpu.get_barrier_semaphore()
    for partner in partners:
        pl.semaphore_signal(barrier, inc=1, device_id=partner, device_id_type=MESH)
    pl.semaphore_wait(barrier, len(partners))

    def from_own(k):
        arrived(f"c{k}", whole_part(k))
        start(f"s{k}")

    def from_other(k):
        arrived(f"s{k}", whole_part(k, 1))

    def before_1():
        for d, place in ((1, 3), (3, 1)):
            arrived(f"b1{d}", unit(f"b0{place}"))
        start("a211", "a213", "b211", "b213", "a2n", "b2n", "a231", "a233", "b231", "b233")
        arrived("a12", unit("a20"))
        start("zb")
        arrived("c1", pair("a01"))
        start("s1", "qz")
        from_other(0)

    def before_2():
        arrived("b12", unit("b02"))
        start("za")
        arrived("c2", pair("b10"))
        start("s2", "qa11", "qa13", "qa12", "a221", "a223", "b221", "b223")
        from_other(1)

    def before_3():
        from_own(3)
        arrived("qz", gather_b.at[0])
        start("qb11", "qb13", "qb12")
        from_other(2)

    def before_4():
        from_own(4)
        start("ta", "tb", "a222", "b222")
        from_other(3)

    def before_5():
        from_own(5)
        arrived("qa1", gather_a.at[pl.ds(1, SIDE - 1)])
        arrived("qb1", gather_b.at[pl.ds(1, SIDE - 1)])
        start("qa22", "qb22", "qas0", "qbs0")
        from_other(4)

    def before_6():
        start("qa21", "qa23", "qb21", "qb23")
        from_own(6)
        from_other(5)

    def before_7():
        from_own(7)
        from_other(6)

    events = (before_1, before_2, before_3, before_4, before_5, before_6, before_7)

    def absorb(slot, piece, count=chunk):
        tile = scores[slot, :count].reshape(count // 8, 8, SLICE)
        columns = slice(piece * SLICE, (piece + 1) * SLICE)
        old = peak[:, columns]
        new = jnp.maximum(old, jnp.max(tile, axis=0))
        added = jnp.sum(jnp.exp(tile - new[None]), axis=0)
        total[:, columns] = total[:, columns] * jnp.exp(old - new) + added
        peak[:, columns] = new

    def score(first, count, before=chunk):
        rows = pl.ds(first, count)
        for piece in range(slices):
            scores[piece % 2, :count] = similar(bank_all[rows, :], refs[piece * SLICE:(piece + 1) * SLICE, :])
            absorb((piece + 1) % 2, (piece - 1) % slices, count if piece else before)

    start("z", "a11", "a13", "a201", "a203", "a12")
    arrived("z", unit("b00"))
    start("b11", "b13")
    for d, place in ((1, 3), (3, 1)):
        arrived(f"a1{d}", unit(f"a{place}0"))
    start("b201", "b203", "b12", "s0")
    load.wait()
    score(0, part)

    def one_chunk(i, carry):
        for k, event in enumerate(events):
            pl.when(i == k)(event)
        score(pl.multiple_of(part + i * chunk, part), chunk)
        return carry

    lax.fori_loop(0, len(events), one_chunk, 0)
    rest = pl.ds(SIDE, plane - SIDE)
    for kind, gather in gathers.items():
        arrived(f"q{kind}2", gather.at[rest])
        start(f"q{kind}s3")
    from_other(len(PARTS) - 1)
    score(first_row(len(PARTS) - 1, 1), part)
    absorb((slices - 1) % 2, slices - 1, part)
    highest = jnp.max(peak[...], axis=0, keepdims=True)
    summed = jnp.sum(total[...] * jnp.exp(peak[...] - highest), axis=0, keepdims=True)
    offset[...] = jnp.broadcast_to(highest + jnp.log(summed), offset.shape)

    quarter = SIDE * q_rows
    for kind, gather in gathers.items():
        arrived(f"q{kind}s0", gather.at[pl.ds(plane, SIDE)])
        arrived(f"q{kind}s3", gather.at[pl.ds(plane + SIDE, plane - SIDE)])
    for k, line in enumerate(BLOCKS):
        for j, gather in enumerate((gather_a, gather_b)):
            for side in range(2):
                first = side * plane + line * SIDE
                rows = join_rows(gather[first:first + SIDE].astype(jnp.float32))
                first = (2 * side + j) * quarter
                q_all[k, first:first + quarter, :] = rows.reshape(quarter, width).astype(jnp.bfloat16)

    def pool(k, carry):
        block = q_all[k]
        for piece in range(slices):
            columns = slice(piece * SLICE, (piece + 1) * SLICE)
            tile = similar(block, refs[columns, :]).reshape(2 * half // 8, 8, SLICE)
            tile = 1.0 / (1.0 + jnp.exp(offset[:, columns][None] - tile))
            weights[:, columns] = tile.reshape(2 * half, SLICE).astype(jnp.bfloat16)
        pooled[k] = jnp.dot(weights[...], refs[...], preferred_element_type=jnp.float32)
        for j in range(SIDE):
            pl.when(k == j)(lambda j=j: after_pool(j))
        return carry

    def after_pool(k):
        start(f"p{k}")
        if k >= 1:
            reduce_block(k - 1)

    def both_cores(k):
        arrived(f"p{k}", from_sib.at[k])
        rows = pooled[k, :half, :] + from_sib[k]
        return [rows[j * quarter:(j + 1) * quarter].reshape(SIDE, q_rows, width) for j in range(2)]

    def reduce_block(k):
        line = BLOCKS[k]
        for rows, send in zip(both_cores(k), (send_a, send_b)):
            send[line - 1] = split_rows(rows).astype(jnp.bfloat16)
        start(f"pa{line}", f"pb{line}")

    lax.fori_loop(0, SIDE, pool, 0)
    same_lo = pl.ds(pl.multiple_of(8 * z_lo, 8), WINDOW)
    other_lo = pl.ds(pl.multiple_of(8 * (1 - z_lo), 8), WINDOW)
    for j, (rows, recv) in enumerate(zip(both_cores(SIDE - 1), (recv_a, recv_b))):
        arrived("pa" if j == 0 else "pb", recv)
        sums[j] = rows + sum(join_rows(recv[d].astype(jnp.float32)) for d in range(SIDE - 1))
        for flip, lo in enumerate((same_lo, other_lo)):
            first = (flip * 2 + j) * SIDE
            windows[first:first + SIDE] = sums[j, :, lo, :].astype(jnp.bfloat16)
    start(*ends)
    rows = sums[0, 0, same_lo, :]
    own = queries[...].astype(jnp.float32)
    own = jnp.where(z_lo == 0, own[:WINDOW], own[q_rows - WINDOW:])
    arrived("f", final.at[pl.ds(1, 4 * SIDE - 1)])
    rows = rows + jnp.sum(final[1:].astype(jnp.float32), axis=0)
    scale = lax.rsqrt(jnp.mean(rows * rows, axis=1, keepdims=True) + 1e-06)
    result = own + rows * scale
    count = out.shape[0]
    out[...] = jnp.where(z_lo == 0, result[:count], result[WINDOW - count:])

    all_sent("u0", bank_all.at[pl.ds(0, 16 * shard)])
    all_sent("u1", bank_all.at[pl.ds(0, (len(unit_sends) - 16) * shard)])
    all_sent("s0", bank_all.at[pl.ds(0, 4 * part)])
    all_sent("s1", bank_all.at[pl.ds(0, 4 * part)])
    all_sent("q", gather_a.at[pl.ds(0, 2 * plane - 1)])
    all_sent("qs", gather_a)
    all_sent("p", from_sib)
    all_sent("pa", send_a)
    all_sent("pb", send_b)
    all_sent("f", final.at[pl.ds(1, 4 * SIDE - 1)])


def per_device(references, bank, queries):
    ref_count, width = references.shape
    shard, q_rows = bank.shape[0], queries.shape[0]
    chunk = 2 * UNITS * shard
    block = 4 * SIDE * q_rows
    unit = (2 * q_rows, width // 2)
    f32, bf16 = jnp.float32, jnp.bfloat16
    return pl.pallas_call(
        kernel,
        out_shape=jax.ShapeDtypeStruct((q_rows // 2, width), f32),
        in_specs=[
            pl.BlockSpec(memory_space=pl.ANY),
            pl.BlockSpec(memory_space=pltpu.VMEM),
            pl.BlockSpec(memory_space=pltpu.VMEM),
        ],
        out_specs=pl.BlockSpec(memory_space=pltpu.VMEM),
        scratch_shapes=[
            pltpu.VMEM((ref_count, width), bf16),
            pltpu.VMEM((len(PARTS) * chunk, width), bf16),
            pltpu.VMEM(unit, bf16),
            pltpu.VMEM((2 * SIDE * SIDE, *unit), bf16),
            pltpu.VMEM((2 * SIDE * SIDE, *unit), bf16),
            pltpu.VMEM((SIDE, block, width), bf16),
            pltpu.VMEM((8, ref_count), f32),
            pltpu.VMEM((8, ref_count), f32),
            pltpu.VMEM((8, ref_count), f32),
            pltpu.VMEM((2, chunk, SLICE), f32),
            pltpu.VMEM((block, ref_count), bf16),
            pltpu.VMEM((SIDE, block, width), f32),
            pltpu.VMEM((SIDE, block // 2, width), f32),
            pltpu.VMEM((SIDE - 1, SIDE, *unit), bf16),
            pltpu.VMEM((SIDE - 1, SIDE, *unit), bf16),
            pltpu.VMEM((SIDE - 1, SIDE, *unit), bf16),
            pltpu.VMEM((SIDE - 1, SIDE, *unit), bf16),
            pltpu.VMEM((2, SIDE, q_rows, width), f32),
            pltpu.VMEM((4 * SIDE, WINDOW, width), bf16),
            pltpu.VMEM((4 * SIDE, WINDOW, width), bf16),
            pltpu.SemaphoreType.DMA,
            pltpu.SemaphoreType.DMA((SEND_SEMS,)),
            pltpu.SemaphoreType.DMA((RECV_SEMS,)),
        ],
        compiler_params=pltpu.CompilerParams(
            collective_id=0, has_side_effects=True, vmem_limit_bytes=56 * 2**20
        ),
    )(references, bank, queries)


def solution(mesh):
    return jax.shard_map(
        per_device,
        mesh=mesh,
        in_specs=(P(("loop", "group"), None), P("loop", None), P("loop", None)),
        out_specs=P(("loop", "group"), None),
        check_vma=False,
    )
```

```python
import jax
import jax.numpy as jnp
from jax import lax
from jax.experimental import pallas as pl
from jax.experimental.pallas import tpu as pltpu
from jax.sharding import PartitionSpec as P

MESH = pl.DeviceIdType.MESH
SIDE = 4
STEPS = (1, 3, 2)
SLICE = 256
LOW = -1e30
BLOCKS = (((2, 0, 4),), ((1, 0, 2), (3, 0, 2)), ((1, 2, 2), (3, 2, 2)), ((0, 0, 4),))


def similar(rows, columns):
    return lax.dot_general(
        rows, columns, (((1,), (1,)), ((), ())), preferred_element_type=jnp.float32
    )


def back(distance):
    return (SIDE - distance) % SIDE


def split_rows(rows):
    half = rows.shape[2] // 2
    return jnp.concatenate([rows[:, :, :half], rows[:, :, half:]], axis=1)


def join_rows(rows):
    half = rows.shape[1] // 2
    return jnp.concatenate([rows[:, :half], rows[:, half:]], axis=2)


PARTS = (
    ("a00", "b00", "a10", "a30"),
    ("a01", "a03", "b01", "b03"),
    ("a20", "b02", "b10", "b30"),
    ("a11", "a13", "b11", "b31"),
    ("a02", "b20", "near a2", "near b2"),
    ("a31", "a33", "b13", "b33"),
    ("a21", "a23", "b12", "b32"),
    ("a22", "b22", "far a2", "far b2"),
)
SLOTS = {name: (k, j) for k, names in enumerate(PARTS) for j, name in enumerate(names)}
UNITS = 4
WINDOW = 16
SEND_SEMS, RECV_SEMS = 12, 40


def kernel(
    refs_hbm, bank, queries, out,
    refs, bank_all, own_q, gather_a, gather_b, q_all,
    peak, total, offset, scores, weights,
    pooled, from_sib, send_a, send_b, recv_a, recv_b, sums, windows, final,
    load_sem, send_sem, recv_sem,
):
    shard, width = bank.shape
    q_rows = queries.shape[0]
    ref_count = refs.shape[0]
    part = UNITS * shard
    chunk = 2 * part
    slices = ref_count // SLICE

    load = pltpu.make_async_copy(refs_hbm, refs, load_sem)
    load.start()

    index, z_lo = lax.axis_index("loop"), lax.axis_index("group")
    core, y = lax.rem(index, 2), lax.rem(index // 2, SIDE)
    x, z_hi = lax.rem(index // (2 * SIDE), SIDE), index // (2 * SIDE * SIDE)

    def device(dx=0, dy=0, flip_hi=0, flip_lo=0, flip_core=0):
        to_x, to_y = lax.rem(x + dx, SIDE), lax.rem(y + dy, SIDE)
        to_hi = 1 - z_hi if flip_hi else z_hi
        to_lo = 1 - z_lo if flip_lo else z_lo
        to_core = 1 - core if flip_core else core
        return (((to_hi * SIDE + to_x) * SIDE + to_y) * 2 + to_core, to_lo)

    sibling = device(flip_core=1)
    twin = device(flip_lo=1)
    facing = device(flip_hi=1, flip_lo=1)
    along_x = {d: device(dx=d) for d in STEPS}
    along_y = {d: device(dy=d) for d in STEPS}

    moves, send_groups, recv_groups = {}, {}, {}

    def group_sem(sems, groups, name):
        return sems.at[groups.setdefault(name, len(groups))]

    def copy(src, dst, sent, landed, target):
        return pltpu.make_async_remote_copy(
            src_ref=src, dst_ref=dst,
            send_sem=group_sem(send_sem, send_groups, sent), recv_sem=group_sem(recv_sem, recv_groups, landed),
            device_id=target, device_id_type=MESH,
        )

    def move(name, src, dst, sent, landed, target):
        moves[name] = lambda: copy(src, dst, sent, landed, target)

    def start(*names):
        for name in names:
            moves[name]().start()

    def arrived(landed, what):
        copy(what, what, next(iter(send_groups)), landed, sibling).wait_recv()

    def all_sent(sent, what):
        copy(what, what, sent, next(iter(recv_groups)), sibling).wait_send()

    def first_row(k, side=0):
        return min((k + 1) * chunk, len(PARTS) * chunk - part) if side else max(k * chunk - part, 0)

    def unit(name):
        k, j = SLOTS[name]
        return bank_all.at[pl.ds(first_row(k) + j * shard, shard)]

    def whole_part(k, side=0):
        return bank_all.at[pl.ds(first_row(k, side), part)]

    def pair(name):
        k, j = SLOTS[name]
        return bank_all.at[pl.ds(first_row(k) + j * shard, 2 * shard)]

    unit_sends = []

    def send_unit(name, src, dst, landed, target):
        move(name, src, unit(dst), f"u{len(unit_sends) // 16}", landed, target)
        unit_sends.append(name)

    send_unit("z", bank, "b00", "z", facing)
    for d in STEPS:
        send_unit(f"a1{d}", bank, f"a{back(d)}0", f"a1{d}", along_x[d])
        send_unit(f"b1{d}", unit("b00"), f"b0{back(d)}", f"b1{d}", along_y[d])
    for place, k_a, k_b in ((0, 1, 2), (1, 3, 3), (3, 5, 5), (2, 6, 6)):
        for d in (1, 3):
            send_unit(f"a2{place}{d}", unit(f"a{place}0") if place else bank, f"a{place}{back(d)}", f"c{k_a}", along_y[d])
            send_unit(f"b2{place}{d}", unit(f"b0{place}"), f"b{back(d)}{place}", f"c{k_b}", along_x[d])

    def near(names):
        k, j = SLOTS[names[0]]
        return bank_all.at[pl.ds(pl.multiple_of(first_row(k) + (j + z_lo) * shard, shard), shard)]

    send_unit("a2n", near(("a10", "a30")), "near a2", "c4", along_y[2])
    send_unit("b2n", near(("b01", "b03")), "near b2", "c4", along_x[2])
    send_unit("za", unit("b02"), "a02", "c4", facing)
    send_unit("zb", unit("a20"), "b20", "c4", facing)
    send_unit("a222", unit("a20"), "a22", "c7", along_y[2])
    send_unit("b222", unit("b02"), "b22", "c7", along_x[2])
    send_unit("ta", unit("near a2"), "far a2", "c7", twin)
    send_unit("tb", unit("near b2"), "far b2", "c7", twin)
    for k in range(len(PARTS)):
        move(f"s{k}", whole_part(k), whole_part(k, 1), f"s{k // 4}", f"s{k}", sibling)

    first_ring = {"a": along_x, "b": along_y}
    second_ring = {"a": along_y, "b": along_x}
    gathers = {"a": gather_a, "b": gather_b}
    plane = SIDE * SIDE
    move("qz", own_q, gather_b.at[0], "q", "qz", facing)
    for kind, gather in gathers.items():
        own = own_q if kind == "a" else gather_b.at[0]
        for d in STEPS:
            move(f"q{kind}1{d}", own, gather.at[back(d)], "q", f"q{kind}1", first_ring[kind][d])
            move(f"q{kind}2{d}", gather.at[pl.ds(0, SIDE)], gather.at[pl.ds(back(d) * SIDE, SIDE)], "q", f"q{kind}2",
                 second_ring[kind][d])
        for name, first, count in (("0", 0, SIDE), ("3", SIDE, plane - SIDE)):
            move(f"q{kind}s{name}", gather.at[pl.ds(first, count)], gather.at[pl.ds(plane + first, count)], "qs",
                 f"q{kind}s{name}", sibling)

    half = 2 * SIDE * q_rows
    for k in range(SIDE):
        move(f"p{k}", pooled.at[k, pl.ds(half, half)], from_sib.at[k], "p", f"p{k}", sibling)
    for runs in BLOCKS[:-1]:
        for d, place, count in runs:
            run = pl.ds(place, count)
            move(f"pa{d}{place}", send_a.at[d - 1, run], recv_a.at[back(d) - 1, run], "pa", "pa", along_y[d])
            move(f"pb{d}{place}", send_b.at[d - 1, run], recv_b.at[back(d) - 1, run], "pb", "pb", along_x[d])
    ends = ([], [])
    for d in range(SIDE):
        for flip in (0, 1):
            for j, target in enumerate((device(dx=d, flip_lo=flip), device(dy=d, flip_hi=1, flip_lo=flip))):
                if d or flip or j:
                    place = (flip * 2 + j) * SIDE
                    move(f"f{place + d}", windows.at[place + d], final.at[place + back(d)], "f", "f", target)
                    ends[j].append(f"f{place + d}")

    bank_all[pl.ds(0, shard), :] = bank[...]
    peak[...] = jnp.full_like(peak, -jnp.inf)
    total[...] = jnp.zeros_like(total)
    scores[1] = jnp.full(scores.shape[1:], LOW, jnp.float32)
    own_q[...] = split_rows(queries[...].astype(jnp.float32)[None])[0].astype(jnp.bfloat16)
    gather_a[0] = own_q[...]

    partners = [sibling, twin, facing, device(flip_hi=1), *along_x.values(), *along_y.values()]
    barrier = pltpu.get_barrier_semaphore()
    for partner in partners:
        pl.semaphore_signal(barrier, inc=1, device_id=partner, device_id_type=MESH)
    pl.semaphore_wait(barrier, len(partners))

    def from_own(k):
        arrived(f"c{k}", whole_part(k))
        start(f"s{k}")

    def from_other(k):
        arrived(f"s{k}", whole_part(k, 1))

    def before_1():
        for d, place in ((1, 3), (3, 1)):
            arrived(f"b1{d}", unit(f"b0{place}"))
        start("a211", "a213", "b211", "b213", "a2n", "b2n", "a231", "a233", "b231", "b233")
        arrived("a12", unit("a20"))
        start("zb")
        arrived("c1", pair("a01"))
        start("s1")
        from_other(0)

    def before_2():
        arrived("b12", unit("b02"))
        start("za")
        arrived("c2", pair("b10"))
        start("s2", "a221", "a223", "b221", "b223")
        from_other(1)

    def before_3():
        from_own(3)
        from_other(2)

    def before_4():
        from_own(4)
        start("ta", "tb", "a222", "b222")
        arrived("qa1", gather_a.at[pl.ds(1, SIDE - 1)])
        arrived("qb1", gather_b.at[pl.ds(1, SIDE - 1)])
        start("qa22", "qb22", "qas0", "qbs0")
        from_other(3)

    def before_5():
        from_own(5)
        start("qa21", "qa23", "qb21", "qb23")
        from_other(4)

    def before_6():
        from_own(6)
        from_other(5)

    def before_7():
        from_own(7)
        from_other(6)

    events = (before_1, before_2, before_3, before_4, before_5, before_6, before_7)

    def absorb(slot, piece, count=chunk):
        tile = scores[slot, :count].reshape(count // 8, 8, SLICE)
        columns = slice(piece * SLICE, (piece + 1) * SLICE)
        old = peak[:, columns]
        new = jnp.maximum(old, jnp.max(tile, axis=0))
        added = jnp.sum(jnp.exp(tile - new[None]), axis=0)
        total[:, columns] = total[:, columns] * jnp.exp(old - new) + added
        peak[:, columns] = new

    def score(first, count, before=chunk):
        rows = pl.ds(first, count)
        for piece in range(slices):
            scores[piece % 2, :count] = similar(bank_all[rows, :], refs[piece * SLICE:(piece + 1) * SLICE, :])
            absorb((piece + 1) % 2, (piece - 1) % slices, count if piece else before)

    start("z", "a11", "a13", "a201", "a203", "qz", "qa11", "qa13")
    arrived("z", unit("b00"))
    start("b11", "b13", "a12", "qa12")
    for d, place in ((1, 3), (3, 1)):
        arrived(f"a1{d}", unit(f"a{place}0"))
    arrived("qz", gather_b.at[0])
    start("b201", "b203", "qb11", "qb13", "b12", "qb12", "s0")
    load.wait()
    score(0, part)

    def one_chunk(i, carry):
        for k, event in enumerate(events):
            pl.when(i == k)(event)
        score(pl.multiple_of(part + i * chunk, part), chunk)
        return carry

    lax.fori_loop(0, len(events), one_chunk, 0)
    rest = pl.ds(SIDE, plane - SIDE)
    for kind, gather in gathers.items():
        arrived(f"q{kind}2", gather.at[rest])
        start(f"q{kind}s3")
    from_other(len(PARTS) - 1)
    score(first_row(len(PARTS) - 1, 1), part)
    absorb((slices - 1) % 2, slices - 1, part)
    highest = jnp.max(peak[...], axis=0, keepdims=True)
    summed = jnp.sum(total[...] * jnp.exp(peak[...] - highest), axis=0, keepdims=True)
    offset[...] = jnp.broadcast_to(highest + jnp.log(summed), offset.shape)

    quarter = SIDE * q_rows
    for kind, gather in gathers.items():
        arrived(f"q{kind}s0", gather.at[pl.ds(plane, SIDE)])
        arrived(f"q{kind}s3", gather.at[pl.ds(plane + SIDE, plane - SIDE)])
    for k, runs in enumerate(BLOCKS):
        for j, gather in enumerate((gather_a, gather_b)):
            for side in range(2):
                row = (2 * side + j) * quarter
                for line, place, count in runs:
                    first = side * plane + line * SIDE + place
                    rows = join_rows(gather[first:first + count].astype(jnp.float32)).astype(jnp.bfloat16)
                    q_all[k, row:row + count * q_rows, :] = rows.reshape(count * q_rows, width)
                    row += count * q_rows

    def pool(k, carry):
        block = q_all[k]
        for piece in range(slices):
            columns = slice(piece * SLICE, (piece + 1) * SLICE)
            tile = similar(block, refs[columns, :]).reshape(2 * half // 8, 8, SLICE)
            tile = 1.0 / (1.0 + jnp.exp(offset[:, columns][None] - tile))
            weights[:, columns] = tile.reshape(2 * half, SLICE).astype(jnp.bfloat16)
        pl.when(k == SIDE - 1)(lambda: reduce_block(SIDE - 2))
        pooled[k] = jnp.dot(weights[...], refs[...], preferred_element_type=jnp.float32)
        for j in range(SIDE):
            pl.when(k == j)(lambda j=j: after_pool(j))
        return carry

    def after_pool(k):
        start(f"p{k}")
        if 1 <= k < SIDE - 1:
            reduce_block(k - 1)

    def both_cores(k):
        arrived(f"p{k}", from_sib.at[k])
        rows = pooled[k, :half, :] + from_sib[k]
        return [rows[j * quarter:(j + 1) * quarter].reshape(SIDE, q_rows, width) for j in range(2)]

    def reduce_block(k):
        for kind, rows, send in zip("ab", both_cores(k), (send_a, send_b)):
            first = 0
            for line, place, count in BLOCKS[k]:
                send[line - 1, place:place + count] = split_rows(rows[first:first + count]).astype(jnp.bfloat16)
                start(f"p{kind}{line}{place}")
                first += count

    lax.fori_loop(0, SIDE, pool, 0)
    same_lo = pl.ds(pl.multiple_of(8 * z_lo, 8), WINDOW)
    other_lo = pl.ds(pl.multiple_of(8 * (1 - z_lo), 8), WINDOW)
    for j, (rows, recv) in enumerate(zip(both_cores(SIDE - 1), (recv_a, recv_b))):
        arrived("pa" if j == 0 else "pb", recv)
        sums[j] = rows + sum(join_rows(recv[d].astype(jnp.float32)) for d in range(SIDE - 1))
        for flip, lo in enumerate((same_lo, other_lo)):
            first = (flip * 2 + j) * SIDE
            windows[first:first + SIDE] = sums[j, :, lo, :].astype(jnp.bfloat16)
        start(*ends[j])
    rows = sums[0, 0, same_lo, :]
    own = queries[...].astype(jnp.float32)
    own = jnp.where(z_lo == 0, own[:WINDOW], own[q_rows - WINDOW:])
    arrived("f", final.at[pl.ds(1, 4 * SIDE - 1)])
    rows = rows + jnp.sum(final[1:].astype(jnp.float32), axis=0)
    scale = lax.rsqrt(jnp.mean(rows * rows, axis=1, keepdims=True) + 1e-06)
    result = own + rows * scale
    count = out.shape[0]
    out[...] = jnp.where(z_lo == 0, result[:count], result[WINDOW - count:])

    all_sent("u0", bank_all.at[pl.ds(0, 16 * shard)])
    all_sent("u1", bank_all.at[pl.ds(0, (len(unit_sends) - 16) * shard)])
    all_sent("s0", bank_all.at[pl.ds(0, 4 * part)])
    all_sent("s1", bank_all.at[pl.ds(0, 4 * part)])
    all_sent("q", gather_a.at[pl.ds(0, 2 * plane - 1)])
    all_sent("qs", gather_a)
    all_sent("p", from_sib)
    all_sent("pa", send_a)
    all_sent("pb", send_b)
    all_sent("f", final.at[pl.ds(1, 4 * SIDE - 1)])


def per_device(references, bank, queries):
    ref_count, width = references.shape
    shard, q_rows = bank.shape[0], queries.shape[0]
    chunk = 2 * UNITS * shard
    block = 4 * SIDE * q_rows
    unit = (2 * q_rows, width // 2)
    f32, bf16 = jnp.float32, jnp.bfloat16
    return pl.pallas_call(
        kernel,
        out_shape=jax.ShapeDtypeStruct((q_rows // 2, width), f32),
        in_specs=[
            pl.BlockSpec(memory_space=pl.ANY),
            pl.BlockSpec(memory_space=pltpu.VMEM),
            pl.BlockSpec(memory_space=pltpu.VMEM),
        ],
        out_specs=pl.BlockSpec(memory_space=pltpu.VMEM),
        scratch_shapes=[
            pltpu.VMEM((ref_count, width), bf16),
            pltpu.VMEM((len(PARTS) * chunk, width), bf16),
            pltpu.VMEM(unit, bf16),
            pltpu.VMEM((2 * SIDE * SIDE, *unit), bf16),
            pltpu.VMEM((2 * SIDE * SIDE, *unit), bf16),
            pltpu.VMEM((SIDE, block, width), bf16),
            pltpu.VMEM((8, ref_count), f32),
            pltpu.VMEM((8, ref_count), f32),
            pltpu.VMEM((8, ref_count), f32),
            pltpu.VMEM((2, chunk, SLICE), f32),
            pltpu.VMEM((block, ref_count), bf16),
            pltpu.VMEM((SIDE, block, width), f32),
            pltpu.VMEM((SIDE, block // 2, width), f32),
            pltpu.VMEM((SIDE - 1, SIDE, *unit), bf16),
            pltpu.VMEM((SIDE - 1, SIDE, *unit), bf16),
            pltpu.VMEM((SIDE - 1, SIDE, *unit), bf16),
            pltpu.VMEM((SIDE - 1, SIDE, *unit), bf16),
            pltpu.VMEM((2, SIDE, q_rows, width), f32),
            pltpu.VMEM((4 * SIDE, WINDOW, width), bf16),
            pltpu.VMEM((4 * SIDE, WINDOW, width), bf16),
            pltpu.SemaphoreType.DMA,
            pltpu.SemaphoreType.DMA((SEND_SEMS,)),
            pltpu.SemaphoreType.DMA((RECV_SEMS,)),
        ],
        compiler_params=pltpu.CompilerParams(
            collective_id=0, has_side_effects=True, vmem_limit_bytes=56 * 2**20
        ),
    )(references, bank, queries)


def solution(mesh):
    return jax.shard_map(
        per_device,
        mesh=mesh,
        in_specs=(P(("loop", "group"), None), P("loop", None), P("loop", None)),
        out_specs=P(("loop", "group"), None),
        check_vma=False,
    )
```

```python
import jax
import jax.numpy as jnp
from jax import lax
from jax.experimental import pallas as pl
from jax.experimental.pallas import tpu as pltpu
from jax.sharding import PartitionSpec as P

MESH = pl.DeviceIdType.MESH
SIDE = 4
STEPS = (1, 3, 2)
SLICE = 256
LOW = -1e30
BLOCKS = (((2, 0, 4),), ((1, 0, 2), (3, 0, 2)), ((1, 2, 2), (3, 2, 2)), ((0, 0, 4),))


def similar(rows, columns):
    return lax.dot_general(
        rows, columns, (((1,), (1,)), ((), ())), preferred_element_type=jnp.float32
    )


def back(distance):
    return (SIDE - distance) % SIDE


def split_rows(rows):
    half = rows.shape[2] // 2
    return jnp.concatenate([rows[:, :, :half], rows[:, :, half:]], axis=1)


def join_rows(rows):
    half = rows.shape[1] // 2
    return jnp.concatenate([rows[:, :half], rows[:, half:]], axis=2)


PARTS = (
    ("a00", "b00", "a10", "a30"),
    ("a01", "a03", "b01", "b03"),
    ("a20", "b02", "b10", "b30"),
    ("a11", "a13", "b11", "b31"),
    ("a02", "b20", "near a2", "near b2"),
    ("a31", "a33", "b13", "b33"),
    ("a21", "a23", "b12", "b32"),
    ("a22", "b22", "far a2", "far b2"),
)
SLOTS = {name: (k, j) for k, names in enumerate(PARTS) for j, name in enumerate(names)}
UNITS = 4
WINDOW = 16
SEND_SEMS, RECV_SEMS = 12, 40


def kernel(
    refs_hbm, bank, queries, out,
    refs, bank_all, own_q, gather_a, gather_b, q_all,
    peak, total, offset, scores, weights,
    pooled, from_sib, send_a, send_b, recv_a, recv_b, sums, windows, final,
    load_sem, send_sem, recv_sem,
):
    shard, width = bank.shape
    q_rows = queries.shape[0]
    ref_count = refs.shape[0]
    part = UNITS * shard
    chunk = 2 * part
    slices = ref_count // SLICE

    load = pltpu.make_async_copy(refs_hbm, refs, load_sem)
    load.start()

    index, z_lo = lax.axis_index("loop"), lax.axis_index("group")
    core, y = lax.rem(index, 2), lax.rem(index // 2, SIDE)
    x, z_hi = lax.rem(index // (2 * SIDE), SIDE), index // (2 * SIDE * SIDE)

    def device(dx=0, dy=0, flip_hi=0, flip_lo=0, flip_core=0):
        to_x, to_y = lax.rem(x + dx, SIDE), lax.rem(y + dy, SIDE)
        to_hi = 1 - z_hi if flip_hi else z_hi
        to_lo = 1 - z_lo if flip_lo else z_lo
        to_core = 1 - core if flip_core else core
        return (((to_hi * SIDE + to_x) * SIDE + to_y) * 2 + to_core, to_lo)

    sibling = device(flip_core=1)
    twin = device(flip_lo=1)
    facing = device(flip_hi=1, flip_lo=1)
    along_x = {d: device(dx=d) for d in STEPS}
    along_y = {d: device(dy=d) for d in STEPS}

    moves, send_groups, recv_groups = {}, {}, {}

    def group_sem(sems, groups, name):
        return sems.at[groups.setdefault(name, len(groups))]

    def copy(src, dst, sent, landed, target):
        return pltpu.make_async_remote_copy(
            src_ref=src, dst_ref=dst,
            send_sem=group_sem(send_sem, send_groups, sent), recv_sem=group_sem(recv_sem, recv_groups, landed),
            device_id=target, device_id_type=MESH,
        )

    def move(name, src, dst, sent, landed, target):
        moves[name] = lambda: copy(src, dst, sent, landed, target)

    def start(*names):
        for name in names:
            moves[name]().start()

    def arrived(landed, what):
        copy(what, what, next(iter(send_groups)), landed, sibling).wait_recv()

    def all_sent(sent, what):
        copy(what, what, sent, next(iter(recv_groups)), sibling).wait_send()

    def first_row(k, side=0):
        return min((k + 1) * chunk, len(PARTS) * chunk - part) if side else max(k * chunk - part, 0)

    def unit(name):
        k, j = SLOTS[name]
        return bank_all.at[pl.ds(first_row(k) + j * shard, shard)]

    def whole_part(k, side=0):
        return bank_all.at[pl.ds(first_row(k, side), part)]

    def pair(name):
        k, j = SLOTS[name]
        return bank_all.at[pl.ds(first_row(k) + j * shard, 2 * shard)]

    unit_sends = []

    def send_unit(name, src, dst, landed, target):
        move(name, src, unit(dst), f"u{len(unit_sends) // 16}", landed, target)
        unit_sends.append(name)

    send_unit("z", bank, "b00", "z", facing)
    for d in STEPS:
        send_unit(f"a1{d}", bank, f"a{back(d)}0", f"a1{d}", along_x[d])
        send_unit(f"b1{d}", unit("b00"), f"b0{back(d)}", f"b1{d}", along_y[d])
    for place, k_a, k_b in ((0, 1, 2), (1, 3, 3), (3, 5, 5), (2, 6, 6)):
        for d in (1, 3):
            send_unit(f"a2{place}{d}", unit(f"a{place}0") if place else bank, f"a{place}{back(d)}", f"c{k_a}", along_y[d])
            send_unit(f"b2{place}{d}", unit(f"b0{place}"), f"b{back(d)}{place}", f"c{k_b}", along_x[d])

    def near(names):
        k, j = SLOTS[names[0]]
        return bank_all.at[pl.ds(pl.multiple_of(first_row(k) + (j + z_lo) * shard, shard), shard)]

    send_unit("a2n", near(("a10", "a30")), "near a2", "c4", along_y[2])
    send_unit("b2n", near(("b01", "b03")), "near b2", "c4", along_x[2])
    send_unit("za", unit("b02"), "a02", "c4", facing)
    send_unit("zb", unit("a20"), "b20", "c4", facing)
    send_unit("a222", unit("a20"), "a22", "c7", along_y[2])
    send_unit("b222", unit("b02"), "b22", "c7", along_x[2])
    send_unit("ta", unit("near a2"), "far a2", "c7", twin)
    send_unit("tb", unit("near b2"), "far b2", "c7", twin)
    for k in range(len(PARTS)):
        move(f"s{k}", whole_part(k), whole_part(k, 1), f"s{k // 4}", f"s{k}", sibling)

    first_ring = {"a": along_x, "b": along_y}
    second_ring = {"a": along_y, "b": along_x}
    gathers = {"a": gather_a, "b": gather_b}
    plane = SIDE * SIDE
    move("qz", own_q, gather_b.at[0], "q", "qz", facing)
    for kind, gather in gathers.items():
        own = own_q if kind == "a" else gather_b.at[0]
        for d in STEPS:
            move(f"q{kind}1{d}", own, gather.at[back(d)], "q", f"q{kind}1", first_ring[kind][d])
            move(f"q{kind}2{d}", gather.at[pl.ds(0, SIDE)], gather.at[pl.ds(back(d) * SIDE, SIDE)], "q", f"q{kind}2",
                 second_ring[kind][d])
        for name, first, count in (("0", 0, SIDE), ("3", SIDE, plane - SIDE)):
            move(f"q{kind}s{name}", gather.at[pl.ds(first, count)], gather.at[pl.ds(plane + first, count)], "qs",
                 f"q{kind}s{name}", sibling)

    half = 2 * SIDE * q_rows
    for k in range(SIDE):
        move(f"p{k}", pooled.at[k, pl.ds(half, half)], from_sib.at[k], "p", f"p{k}", sibling)
    for runs in BLOCKS[:-1]:
        for d, place, count in runs:
            run = pl.ds(place, count)
            move(f"pa{d}{place}", send_a.at[d - 1, run], recv_a.at[back(d) - 1, run], "pa", "pa", along_y[d])
            move(f"pb{d}{place}", send_b.at[d - 1, run], recv_b.at[back(d) - 1, run], "pb", "pb", along_x[d])
    ends = ([], [])
    for d in range(SIDE):
        for flip in (0, 1):
            for j, target in enumerate((device(dx=d, flip_lo=flip), device(dy=d, flip_hi=1, flip_lo=flip))):
                if d or flip or j:
                    place = (flip * 2 + j) * SIDE
                    move(f"f{place + d}", windows.at[place + d], final.at[place + back(d)], "f", "f", target)
                    ends[j].append(f"f{place + d}")

    bank_all[pl.ds(0, shard), :] = bank[...]
    peak[...] = jnp.full_like(peak, -jnp.inf)
    total[...] = jnp.zeros_like(total)
    scores[1] = jnp.full(scores.shape[1:], LOW, jnp.float32)
    own_q[...] = split_rows(queries[...].astype(jnp.float32)[None])[0].astype(jnp.bfloat16)
    gather_a[0] = own_q[...]

    partners = [sibling, twin, facing, device(flip_hi=1), *along_x.values(), *along_y.values()]
    barrier = pltpu.get_barrier_semaphore()
    for partner in partners:
        pl.semaphore_signal(barrier, inc=1, device_id=partner, device_id_type=MESH)
    pl.semaphore_wait(barrier, len(partners))

    def from_own(k):
        arrived(f"c{k}", whole_part(k))
        start(f"s{k}")

    def from_other(k):
        arrived(f"s{k}", whole_part(k, 1))

    def before_1():
        for d, place in ((1, 3), (3, 1)):
            arrived(f"b1{d}", unit(f"b0{place}"))
        start("a211", "a213", "b211", "b213", "a2n", "b2n")
        arrived("a12", unit("a20"))
        start("zb")
        arrived("c1", pair("a01"))
        start("s1")
        from_other(0)

    def before_2():
        arrived("b12", unit("b02"))
        start("za", "a231", "a233", "b231", "b233")
        arrived("c2", pair("b10"))
        start("s2", "a221", "a223", "b221", "b223")
        from_other(1)

    def before_3():
        from_own(3)
        from_other(2)

    def before_4():
        from_own(4)
        start("ta", "tb", "a222", "b222")
        arrived("qa1", gather_a.at[pl.ds(1, SIDE - 1)])
        arrived("qb1", gather_b.at[pl.ds(1, SIDE - 1)])
        start("qa22", "qb22", "qas0", "qbs0")
        from_other(3)

    def before_5():
        from_own(5)
        start("qa21", "qa23", "qb21", "qb23")
        from_other(4)

    def before_6():
        from_own(6)
        from_other(5)

    def before_7():
        from_own(7)
        from_other(6)

    events = (before_1, before_2, before_3, before_4, before_5, before_6, before_7)

    def absorb(slot, piece, count=chunk):
        tile = scores[slot, :count].reshape(count // 8, 8, SLICE)
        columns = slice(piece * SLICE, (piece + 1) * SLICE)
        old = peak[:, columns]
        new = jnp.maximum(old, jnp.max(tile, axis=0))
        added = jnp.sum(jnp.exp(tile - new[None]), axis=0)
        total[:, columns] = total[:, columns] * jnp.exp(old - new) + added
        peak[:, columns] = new

    def score(first, count, before=chunk):
        rows = pl.ds(first, count)
        for piece in range(slices):
            scores[piece % 2, :count] = similar(bank_all[rows, :], refs[piece * SLICE:(piece + 1) * SLICE, :])
            absorb((piece + 1) % 2, (piece - 1) % slices, count if piece else before)

    start("z", "a11", "a13", "a201", "a203", "qz", "qa11", "qa13")
    arrived("z", unit("b00"))
    start("b11", "b13", "a12", "qa12")
    for d, place in ((1, 3), (3, 1)):
        arrived(f"a1{d}", unit(f"a{place}0"))
    arrived("qz", gather_b.at[0])
    start("b201", "b203", "qb11", "qb13", "b12", "qb12", "s0")
    load.wait()
    score(0, part)

    def one_chunk(i, carry):
        for k, event in enumerate(events):
            pl.when(i == k)(event)
        score(pl.multiple_of(part + i * chunk, part), chunk)
        return carry

    lax.fori_loop(0, len(events), one_chunk, 0)
    rest = pl.ds(SIDE, plane - SIDE)
    for kind, gather in gathers.items():
        arrived(f"q{kind}2", gather.at[rest])
        start(f"q{kind}s3")
    from_other(len(PARTS) - 1)
    score(first_row(len(PARTS) - 1, 1), part)
    absorb((slices - 1) % 2, slices - 1, part)
    highest = jnp.max(peak[...], axis=0, keepdims=True)
    summed = jnp.sum(total[...] * jnp.exp(peak[...] - highest), axis=0, keepdims=True)
    offset[...] = jnp.broadcast_to(highest + jnp.log(summed), offset.shape)

    quarter = SIDE * q_rows
    for kind, gather in gathers.items():
        arrived(f"q{kind}s0", gather.at[pl.ds(plane, SIDE)])
        arrived(f"q{kind}s3", gather.at[pl.ds(plane + SIDE, plane - SIDE)])
    for k, runs in enumerate(BLOCKS):
        for j, gather in enumerate((gather_a, gather_b)):
            for side in range(2):
                row = (2 * side + j) * quarter
                for line, place, count in runs:
                    first = side * plane + line * SIDE + place
                    rows = join_rows(gather[first:first + count].astype(jnp.float32)).astype(jnp.bfloat16)
                    q_all[k, row:row + count * q_rows, :] = rows.reshape(count * q_rows, width)
                    row += count * q_rows

    def pool(k):
        block = q_all[k]
        for piece in range(slices):
            columns = slice(piece * SLICE, (piece + 1) * SLICE)
            tile = similar(block, refs[columns, :]).reshape(2 * half // 8, 8, SLICE)
            tile = 1.0 / (1.0 + jnp.exp(offset[:, columns][None] - tile))
            weights[:, columns] = tile.reshape(2 * half, SLICE).astype(jnp.bfloat16)
        if k == SIDE - 1:
            reduce_block(SIDE - 2)
        pooled[k] = jnp.dot(weights[...], refs[...], preferred_element_type=jnp.float32)
        after_pool(k)

    def after_pool(k):
        start(f"p{k}")
        if 1 <= k < SIDE - 1:
            reduce_block(k - 1)

    def both_cores(k):
        arrived(f"p{k}", from_sib.at[k])
        rows = pooled[k, :half, :] + from_sib[k]
        return [rows[j * quarter:(j + 1) * quarter].reshape(SIDE, q_rows, width) for j in range(2)]

    def reduce_block(k):
        for kind, rows, send in zip("ab", both_cores(k), (send_a, send_b)):
            first = 0
            for line, place, count in BLOCKS[k]:
                send[line - 1, place:place + count] = split_rows(rows[first:first + count]).astype(jnp.bfloat16)
                start(f"p{kind}{line}{place}")
                first += count

    for k in range(SIDE):
        pool(k)
    same_lo = pl.ds(pl.multiple_of(8 * z_lo, 8), WINDOW)
    other_lo = pl.ds(pl.multiple_of(8 * (1 - z_lo), 8), WINDOW)
    for j, (rows, recv) in enumerate(zip(both_cores(SIDE - 1), (recv_a, recv_b))):
        arrived("pa" if j == 0 else "pb", recv)
        sums[j] = rows + sum(join_rows(recv[d].astype(jnp.float32)) for d in range(SIDE - 1))
        for flip, lo in enumerate((same_lo, other_lo)):
            first = (flip * 2 + j) * SIDE
            windows[first:first + SIDE] = sums[j, :, lo, :].astype(jnp.bfloat16)
        start(*ends[j])
    rows = sums[0, 0, same_lo, :]
    own = queries[...].astype(jnp.float32)
    own = jnp.where(z_lo == 0, own[:WINDOW], own[q_rows - WINDOW:])
    arrived("f", final.at[pl.ds(1, 4 * SIDE - 1)])
    rows = rows + jnp.sum(final[1:].astype(jnp.float32), axis=0)
    scale = lax.rsqrt(jnp.mean(rows * rows, axis=1, keepdims=True) + 1e-06)
    result = own + rows * scale
    count = out.shape[0]
    out[...] = jnp.where(z_lo == 0, result[:count], result[WINDOW - count:])

    all_sent("u0", bank_all.at[pl.ds(0, 16 * shard)])
    all_sent("u1", bank_all.at[pl.ds(0, (len(unit_sends) - 16) * shard)])
    all_sent("s0", bank_all.at[pl.ds(0, 4 * part)])
    all_sent("s1", bank_all.at[pl.ds(0, 4 * part)])
    all_sent("q", gather_a.at[pl.ds(0, 2 * plane - 1)])
    all_sent("qs", gather_a)
    all_sent("p", from_sib)
    all_sent("pa", send_a)
    all_sent("pb", send_b)
    all_sent("f", final.at[pl.ds(1, 4 * SIDE - 1)])


def per_device(references, bank, queries):
    ref_count, width = references.shape
    shard, q_rows = bank.shape[0], queries.shape[0]
    chunk = 2 * UNITS * shard
    block = 4 * SIDE * q_rows
    unit = (2 * q_rows, width // 2)
    f32, bf16 = jnp.float32, jnp.bfloat16
    return pl.pallas_call(
        kernel,
        out_shape=jax.ShapeDtypeStruct((q_rows // 2, width), f32),
        in_specs=[
            pl.BlockSpec(memory_space=pl.ANY),
            pl.BlockSpec(memory_space=pltpu.VMEM),
            pl.BlockSpec(memory_space=pltpu.VMEM),
        ],
        out_specs=pl.BlockSpec(memory_space=pltpu.VMEM),
        scratch_shapes=[
            pltpu.VMEM((ref_count, width), bf16),
            pltpu.VMEM((len(PARTS) * chunk, width), bf16),
            pltpu.VMEM(unit, bf16),
            pltpu.VMEM((2 * SIDE * SIDE, *unit), bf16),
            pltpu.VMEM((2 * SIDE * SIDE, *unit), bf16),
            pltpu.VMEM((SIDE, block, width), bf16),
            pltpu.VMEM((8, ref_count), f32),
            pltpu.VMEM((8, ref_count), f32),
            pltpu.VMEM((8, ref_count), f32),
            pltpu.VMEM((2, chunk, SLICE), f32),
            pltpu.VMEM((block, ref_count), bf16),
            pltpu.VMEM((SIDE, block, width), f32),
            pltpu.VMEM((SIDE, block // 2, width), f32),
            pltpu.VMEM((SIDE - 1, SIDE, *unit), bf16),
            pltpu.VMEM((SIDE - 1, SIDE, *unit), bf16),
            pltpu.VMEM((SIDE - 1, SIDE, *unit), bf16),
            pltpu.VMEM((SIDE - 1, SIDE, *unit), bf16),
            pltpu.VMEM((2, SIDE, q_rows, width), f32),
            pltpu.VMEM((4 * SIDE, WINDOW, width), bf16),
            pltpu.VMEM((4 * SIDE, WINDOW, width), bf16),
            pltpu.SemaphoreType.DMA,
            pltpu.SemaphoreType.DMA((SEND_SEMS,)),
            pltpu.SemaphoreType.DMA((RECV_SEMS,)),
        ],
        compiler_params=pltpu.CompilerParams(
            collective_id=0, has_side_effects=True, vmem_limit_bytes=56 * 2**20
        ),
    )(references, bank, queries)


def solution(mesh):
    return jax.shard_map(
        per_device,
        mesh=mesh,
        in_specs=(P(("loop", "group"), None), P("loop", None), P("loop", None)),
        out_specs=P(("loop", "group"), None),
        check_vma=False,
    )
```

```python
import jax
import jax.numpy as jnp
from jax import lax
from jax.experimental import pallas as pl
from jax.experimental.pallas import tpu as pltpu
from jax.sharding import PartitionSpec as P

MESH = pl.DeviceIdType.MESH
SIDE = 4
STEPS = (1, 3, 2)
SLICE = 256
LOW = -1e30
BLOCKS = (((2, 0, 4),), ((1, 0, 2), (3, 0, 2)), ((1, 2, 2), (3, 2, 2)), ((0, 0, 4),))


def similar(rows, columns):
    return lax.dot_general(
        rows, columns, (((1,), (1,)), ((), ())), preferred_element_type=jnp.float32
    )


def back(distance):
    return (SIDE - distance) % SIDE


def split_rows(rows):
    half = rows.shape[2] // 2
    return jnp.concatenate([rows[:, :, :half], rows[:, :, half:]], axis=1)


def join_rows(rows):
    half = rows.shape[1] // 2
    return jnp.concatenate([rows[:, :half], rows[:, half:]], axis=2)


PARTS = (
    ("a00", "b00", "a10", "a30"),
    ("a01", "a03", "b01", "b03"),
    ("a20", "b02", "b10", "b30"),
    ("a11", "a13", "b11", "b31"),
    ("a02", "b20", "near a2", "near b2"),
    ("a31", "a33", "b13", "b33"),
    ("a21", "a23", "b12", "b32"),
    ("a22", "b22", "far a2", "far b2"),
)
SLOTS = {name: (k, j) for k, names in enumerate(PARTS) for j, name in enumerate(names)}
UNITS = 4
WINDOW = 16
SEND_SEMS, RECV_SEMS = 12, 40


def kernel(
    refs_hbm, bank, queries, out,
    refs, bank_all, own_q, gather_a, gather_b, q_all,
    peak, total, offset, scores, weights,
    pooled, from_sib, send_a, send_b, recv_a, recv_b, sums, windows, final,
    load_sem, send_sem, recv_sem,
):
    shard, width = bank.shape
    q_rows = queries.shape[0]
    ref_count = refs.shape[0]
    part = UNITS * shard
    chunk = 2 * part
    slices = ref_count // SLICE

    load = pltpu.make_async_copy(refs_hbm, refs, load_sem)
    load.start()

    index, z_lo = lax.axis_index("loop"), lax.axis_index("group")
    core, y = lax.rem(index, 2), lax.rem(index // 2, SIDE)
    x, z_hi = lax.rem(index // (2 * SIDE), SIDE), index // (2 * SIDE * SIDE)

    def device(dx=0, dy=0, flip_hi=0, flip_lo=0, flip_core=0):
        to_x, to_y = lax.rem(x + dx, SIDE), lax.rem(y + dy, SIDE)
        to_hi = 1 - z_hi if flip_hi else z_hi
        to_lo = 1 - z_lo if flip_lo else z_lo
        to_core = 1 - core if flip_core else core
        return (((to_hi * SIDE + to_x) * SIDE + to_y) * 2 + to_core, to_lo)

    sibling = device(flip_core=1)
    twin = device(flip_lo=1)
    facing = device(flip_hi=1, flip_lo=1)
    along_x = {d: device(dx=d) for d in STEPS}
    along_y = {d: device(dy=d) for d in STEPS}

    moves, send_groups, recv_groups = {}, {}, {}

    def group_sem(sems, groups, name):
        return sems.at[groups.setdefault(name, len(groups))]

    def copy(src, dst, sent, landed, target):
        return pltpu.make_async_remote_copy(
            src_ref=src, dst_ref=dst,
            send_sem=group_sem(send_sem, send_groups, sent), recv_sem=group_sem(recv_sem, recv_groups, landed),
            device_id=target, device_id_type=MESH,
        )

    def move(name, src, dst, sent, landed, target):
        moves[name] = lambda: copy(src, dst, sent, landed, target)

    def start(*names):
        for name in names:
            moves[name]().start()

    def arrived(landed, what):
        copy(what, what, next(iter(send_groups)), landed, sibling).wait_recv()

    def all_sent(sent, what):
        copy(what, what, sent, next(iter(recv_groups)), sibling).wait_send()

    def first_row(k, side=0):
        return min((k + 1) * chunk, len(PARTS) * chunk - part) if side else max(k * chunk - part, 0)

    def unit(name):
        k, j = SLOTS[name]
        return bank_all.at[pl.ds(first_row(k) + j * shard, shard)]

    def whole_part(k, side=0):
        return bank_all.at[pl.ds(first_row(k, side), part)]

    def pair(name):
        k, j = SLOTS[name]
        return bank_all.at[pl.ds(first_row(k) + j * shard, 2 * shard)]

    unit_sends = []

    def send_unit(name, src, dst, landed, target):
        move(name, src, unit(dst), f"u{len(unit_sends) // 16}", landed, target)
        unit_sends.append(name)

    send_unit("z", bank, "b00", "z", facing)
    for d in STEPS:
        send_unit(f"a1{d}", bank, f"a{back(d)}0", f"a1{d}", along_x[d])
        send_unit(f"b1{d}", unit("b00"), f"b0{back(d)}", f"b1{d}", along_y[d])
    for place, k_a, k_b in ((0, 1, 2), (1, 3, 3), (3, 5, 5), (2, 6, 6)):
        for d in (1, 3):
            send_unit(f"a2{place}{d}", unit(f"a{place}0") if place else bank, f"a{place}{back(d)}", f"c{k_a}", along_y[d])
            send_unit(f"b2{place}{d}", unit(f"b0{place}"), f"b{back(d)}{place}", f"c{k_b}", along_x[d])

    def near(names):
        k, j = SLOTS[names[0]]
        return bank_all.at[pl.ds(pl.multiple_of(first_row(k) + (j + z_lo) * shard, shard), shard)]

    send_unit("a2n", near(("a10", "a30")), "near a2", "c4", along_y[2])
    send_unit("b2n", near(("b01", "b03")), "near b2", "c4", along_x[2])
    send_unit("za", unit("b02"), "a02", "c4", facing)
    send_unit("zb", unit("a20"), "b20", "c4", facing)
    send_unit("a222", unit("a20"), "a22", "c7", along_y[2])
    send_unit("b222", unit("b02"), "b22", "c7", along_x[2])
    send_unit("ta", unit("near a2"), "far a2", "c7", twin)
    send_unit("tb", unit("near b2"), "far b2", "c7", twin)
    for k in range(len(PARTS)):
        move(f"s{k}", whole_part(k), whole_part(k, 1), f"s{k // 4}", f"s{k}", sibling)

    first_ring = {"a": along_x, "b": along_y}
    second_ring = {"a": along_y, "b": along_x}
    gathers = {"a": gather_a, "b": gather_b}
    plane = SIDE * SIDE
    move("qz", own_q, gather_b.at[0], "q", "qz", facing)
    for kind, gather in gathers.items():
        own = own_q if kind == "a" else gather_b.at[0]
        for d in STEPS:
            move(f"q{kind}1{d}", own, gather.at[back(d)], "q", f"q{kind}1", first_ring[kind][d])
            move(f"q{kind}2{d}", gather.at[pl.ds(0, SIDE)], gather.at[pl.ds(back(d) * SIDE, SIDE)], "q", f"q{kind}2",
                 second_ring[kind][d])
        for name, first, count in (("0", 0, SIDE), ("3", SIDE, plane - SIDE)):
            move(f"q{kind}s{name}", gather.at[pl.ds(first, count)], gather.at[pl.ds(plane + first, count)], "qs",
                 f"q{kind}s{name}", sibling)

    half = 2 * SIDE * q_rows
    for k in range(SIDE):
        move(f"p{k}", pooled.at[k, pl.ds(half, half)], from_sib.at[k], "p", f"p{k}", sibling)
    for runs in BLOCKS[:-1]:
        for d, place, count in runs:
            run = pl.ds(place, count)
            move(f"pa{d}{place}", send_a.at[d - 1, run], recv_a.at[back(d) - 1, run], "pa", "pa", along_y[d])
            move(f"pb{d}{place}", send_b.at[d - 1, run], recv_b.at[back(d) - 1, run], "pb", "pb", along_x[d])
    ends = ([], [])
    for d in range(SIDE):
        for flip in (0, 1):
            for j, target in enumerate((device(dx=d, flip_lo=flip), device(dy=d, flip_hi=1, flip_lo=flip))):
                if d or flip or j:
                    place = (flip * 2 + j) * SIDE
                    move(f"f{place + d}", windows.at[place + d], final.at[place + back(d)], "f", "f", target)
                    ends[j].append(f"f{place + d}")

    partners = [sibling, twin, facing, device(flip_hi=1), *along_x.values(), *along_y.values()]
    barrier = pltpu.get_barrier_semaphore()
    for partner in partners:
        pl.semaphore_signal(barrier, inc=1, device_id=partner, device_id_type=MESH)

    bank_all[pl.ds(0, shard), :] = bank[...]
    peak[...] = jnp.full_like(peak, -jnp.inf)
    total[...] = jnp.zeros_like(total)
    scores[1] = jnp.full(scores.shape[1:], LOW, jnp.float32)
    own_q[...] = split_rows(queries[...].astype(jnp.float32)[None])[0].astype(jnp.bfloat16)
    gather_a[0] = own_q[...]
    pl.semaphore_wait(barrier, len(partners))

    def from_own(k):
        arrived(f"c{k}", whole_part(k))
        start(f"s{k}")

    def from_other(k):
        arrived(f"s{k}", whole_part(k, 1))

    def before_1():
        for d, place in ((1, 3), (3, 1)):
            arrived(f"b1{d}", unit(f"b0{place}"))
        start("a211", "a213", "b211", "b213", "a2n", "b2n")
        arrived("a12", unit("a20"))
        start("zb")
        arrived("c1", pair("a01"))
        start("s1")
        from_other(0)

    def before_2():
        arrived("b12", unit("b02"))
        start("za", "a231", "a233", "b231", "b233")
        arrived("c2", pair("b10"))
        start("s2", "a221", "a223", "b221", "b223")
        from_other(1)

    def before_3():
        from_own(3)
        from_other(2)

    def before_4():
        from_own(4)
        start("ta", "tb", "a222", "b222")
        arrived("qa1", gather_a.at[pl.ds(1, SIDE - 1)])
        arrived("qb1", gather_b.at[pl.ds(1, SIDE - 1)])
        start("qa22", "qb22", "qas0", "qbs0")
        from_other(3)

    def before_5():
        from_own(5)
        start("qa21", "qa23", "qb21", "qb23")
        from_other(4)

    def before_6():
        from_own(6)
        from_other(5)

    def before_7():
        from_own(7)
        from_other(6)

    events = (before_1, before_2, before_3, before_4, before_5, before_6, before_7)

    def absorb(slot, piece, count=chunk):
        tile = scores[slot, :count].reshape(count // 8, 8, SLICE)
        columns = slice(piece * SLICE, (piece + 1) * SLICE)
        old = peak[:, columns]
        new = jnp.maximum(old, jnp.max(tile, axis=0))
        added = jnp.sum(jnp.exp(tile - new[None]), axis=0)
        total[:, columns] = total[:, columns] * jnp.exp(old - new) + added
        peak[:, columns] = new

    def score(first, count, before=chunk):
        rows = pl.ds(first, count)
        for piece in range(slices):
            scores[piece % 2, :count] = similar(bank_all[rows, :], refs[piece * SLICE:(piece + 1) * SLICE, :])
            absorb((piece + 1) % 2, (piece - 1) % slices, count if piece else before)

    start("z", "a11", "a13", "a201", "a203", "qz", "qa11", "qa13")
    arrived("z", unit("b00"))
    start("b11", "b13", "a12", "qa12")
    for d, place in ((1, 3), (3, 1)):
        arrived(f"a1{d}", unit(f"a{place}0"))
    arrived("qz", gather_b.at[0])
    start("b201", "b203", "qb11", "qb13", "b12", "qb12", "s0")
    load.wait()
    score(0, part)

    def one_chunk(i, carry):
        for k, event in enumerate(events):
            pl.when(i == k)(event)
        score(pl.multiple_of(part + i * chunk, part), chunk)
        return carry

    lax.fori_loop(0, len(events), one_chunk, 0)
    rest = pl.ds(SIDE, plane - SIDE)
    for kind, gather in gathers.items():
        arrived(f"q{kind}2", gather.at[rest])
        start(f"q{kind}s3")
    from_other(len(PARTS) - 1)
    score(first_row(len(PARTS) - 1, 1), part)
    absorb((slices - 1) % 2, slices - 1, part)
    highest = jnp.max(peak[...], axis=0, keepdims=True)
    summed = jnp.sum(total[...] * jnp.exp(peak[...] - highest), axis=0, keepdims=True)
    offset[...] = jnp.broadcast_to(highest + jnp.log(summed), offset.shape)

    quarter = SIDE * q_rows
    for kind, gather in gathers.items():
        arrived(f"q{kind}s0", gather.at[pl.ds(plane, SIDE)])
        arrived(f"q{kind}s3", gather.at[pl.ds(plane + SIDE, plane - SIDE)])
    for k, runs in enumerate(BLOCKS):
        for j, gather in enumerate((gather_a, gather_b)):
            for side in range(2):
                row = (2 * side + j) * quarter
                for line, place, count in runs:
                    first = side * plane + line * SIDE + place
                    rows = join_rows(gather[first:first + count].astype(jnp.float32)).astype(jnp.bfloat16)
                    q_all[k, row:row + count * q_rows, :] = rows.reshape(count * q_rows, width)
                    row += count * q_rows

    def pool(k):
        block = q_all[k]
        for piece in range(slices):
            columns = slice(piece * SLICE, (piece + 1) * SLICE)
            tile = similar(block, refs[columns, :]).reshape(2 * half // 8, 8, SLICE)
            tile = 1.0 / (1.0 + jnp.exp(offset[:, columns][None] - tile))
            weights[:, columns] = tile.reshape(2 * half, SLICE).astype(jnp.bfloat16)
        if k == SIDE - 1:
            reduce_block(SIDE - 2)
        pooled[k] = jnp.dot(weights[...], refs[...], preferred_element_type=jnp.float32)
        after_pool(k)

    def after_pool(k):
        start(f"p{k}")
        if 1 <= k < SIDE - 1:
            reduce_block(k - 1)

    def both_cores(k):
        arrived(f"p{k}", from_sib.at[k])
        rows = pooled[k, :half, :] + from_sib[k]
        return [rows[j * quarter:(j + 1) * quarter].reshape(SIDE, q_rows, width) for j in range(2)]

    def reduce_block(k):
        for kind, rows, send in zip("ab", both_cores(k), (send_a, send_b)):
            first = 0
            for line, place, count in BLOCKS[k]:
                send[line - 1, place:place + count] = split_rows(rows[first:first + count]).astype(jnp.bfloat16)
                start(f"p{kind}{line}{place}")
                first += count

    for k in range(SIDE):
        pool(k)
    same_lo = pl.ds(pl.multiple_of(8 * z_lo, 8), WINDOW)
    other_lo = pl.ds(pl.multiple_of(8 * (1 - z_lo), 8), WINDOW)
    for j, (rows, recv) in enumerate(zip(both_cores(SIDE - 1), (recv_a, recv_b))):
        arrived("pa" if j == 0 else "pb", recv)
        sums[j] = rows + sum(join_rows(recv[d].astype(jnp.float32)) for d in range(SIDE - 1))
        for flip, lo in enumerate((same_lo, other_lo)):
            first = (flip * 2 + j) * SIDE
            windows[first:first + SIDE] = sums[j, :, lo, :].astype(jnp.bfloat16)
        start(*ends[j])
    rows = sums[0, 0, same_lo, :]
    own = queries[...].astype(jnp.float32)
    own = jnp.where(z_lo == 0, own[:WINDOW], own[q_rows - WINDOW:])
    arrived("f", final.at[pl.ds(1, 4 * SIDE - 1)])
    rows = rows + jnp.sum(final[1:].astype(jnp.float32), axis=0)
    scale = lax.rsqrt(jnp.mean(rows * rows, axis=1, keepdims=True) + 1e-06)
    result = own + rows * scale
    count = out.shape[0]
    out[...] = jnp.where(z_lo == 0, result[:count], result[WINDOW - count:])

    all_sent("u0", bank_all.at[pl.ds(0, 16 * shard)])
    all_sent("u1", bank_all.at[pl.ds(0, (len(unit_sends) - 16) * shard)])
    all_sent("s0", bank_all.at[pl.ds(0, 4 * part)])
    all_sent("s1", bank_all.at[pl.ds(0, 4 * part)])
    all_sent("q", gather_a.at[pl.ds(0, 2 * plane - 1)])
    all_sent("qs", gather_a)
    all_sent("p", from_sib)
    all_sent("pa", send_a)
    all_sent("pb", send_b)
    all_sent("f", final.at[pl.ds(1, 4 * SIDE - 1)])


def per_device(references, bank, queries):
    ref_count, width = references.shape
    shard, q_rows = bank.shape[0], queries.shape[0]
    chunk = 2 * UNITS * shard
    block = 4 * SIDE * q_rows
    unit = (2 * q_rows, width // 2)
    f32, bf16 = jnp.float32, jnp.bfloat16
    return pl.pallas_call(
        kernel,
        out_shape=jax.ShapeDtypeStruct((q_rows // 2, width), f32),
        in_specs=[
            pl.BlockSpec(memory_space=pl.ANY),
            pl.BlockSpec(memory_space=pltpu.VMEM),
            pl.BlockSpec(memory_space=pltpu.VMEM),
        ],
        out_specs=pl.BlockSpec(memory_space=pltpu.VMEM),
        scratch_shapes=[
            pltpu.VMEM((ref_count, width), bf16),
            pltpu.VMEM((len(PARTS) * chunk, width), bf16),
            pltpu.VMEM(unit, bf16),
            pltpu.VMEM((2 * SIDE * SIDE, *unit), bf16),
            pltpu.VMEM((2 * SIDE * SIDE, *unit), bf16),
            pltpu.VMEM((SIDE, block, width), bf16),
            pltpu.VMEM((8, ref_count), f32),
            pltpu.VMEM((8, ref_count), f32),
            pltpu.VMEM((8, ref_count), f32),
            pltpu.VMEM((2, chunk, SLICE), f32),
            pltpu.VMEM((block, ref_count), bf16),
            pltpu.VMEM((SIDE, block, width), f32),
            pltpu.VMEM((SIDE, block // 2, width), f32),
            pltpu.VMEM((SIDE - 1, SIDE, *unit), bf16),
            pltpu.VMEM((SIDE - 1, SIDE, *unit), bf16),
            pltpu.VMEM((SIDE - 1, SIDE, *unit), bf16),
            pltpu.VMEM((SIDE - 1, SIDE, *unit), bf16),
            pltpu.VMEM((2, SIDE, q_rows, width), f32),
            pltpu.VMEM((4 * SIDE, WINDOW, width), bf16),
            pltpu.VMEM((4 * SIDE, WINDOW, width), bf16),
            pltpu.SemaphoreType.DMA,
            pltpu.SemaphoreType.DMA((SEND_SEMS,)),
            pltpu.SemaphoreType.DMA((RECV_SEMS,)),
        ],
        compiler_params=pltpu.CompilerParams(
            collective_id=0, has_side_effects=True, vmem_limit_bytes=56 * 2**20
        ),
    )(references, bank, queries)


def solution(mesh):
    return jax.shard_map(
        per_device,
        mesh=mesh,
        in_specs=(P(("loop", "group"), None), P("loop", None), P("loop", None)),
        out_specs=P(("loop", "group"), None),
        check_vma=False,
    )
```
